32 devices in a mesh: group: 4 (over y, x), dom: 8 (over z, core).
Axes of the slice: x: 2, y: 2, z: 4, core: 2. Of those that a mesh axis runs over, the one named last changes fastest.
Arguments:
- node_lat: bfloat16 [65536, 256], P(('group', 'dom')), may hold values from -6 to 6
- edge_lat: bfloat16 [262144, 256], P(('group', 'dom')), may hold values from -6 to 6
- edge_send: int32 [262144], P(('group', 'dom')), may hold values from 0 to 3071, as said below
- halo_list: int32 [32768], P(('group', 'dom')), may hold values from 0 to 2047
- pool_id: int32 [65536], P(('group', 'dom')), may hold values from 0 to 1023
- coarse_lat: bfloat16 [8192, 256], P(('group', 'dom')), may hold values from -6 to 6
- cedge_lat: bfloat16 [32768, 256], P(('group', 'dom')), may hold values from -6 to 6
- cedge_send: int32 [32768], P(('group', 'dom')), may hold values from 0 to 511, as said below
- chalo_list: int32 [8192], P(('group', 'dom')), may hold values from 0 to 255
- fine_edge_in: bfloat16 [3, 256, 256], replicated, may hold values from -0.21875 to 0.21875
- fine_edge_out: bfloat16 [256, 256], replicated, may hold values from -0.375 to 0.375
- fine_node_in: bfloat16 [2, 256, 256], replicated, may hold values from -0.25 to 0.25
- fine_node_out: bfloat16 [256, 256], replicated, may hold values from -0.375 to 0.375
- fine_bias: float32 [4, 256], replicated, may hold values from -3 to 3
- fine_gain: float32 [2, 256], replicated, may hold values from 0.1 to 1.9
- coarse_edge_in: bfloat16 [3, 256, 256], replicated, may hold values from -0.21875 to 0.21875
- coarse_edge_out: bfloat16 [256, 256], replicated, may hold values from -0.375 to 0.375
- coarse_node_in: bfloat16 [2, 256, 256], replicated, may hold values from -0.25 to 0.25
- coarse_node_out: bfloat16 [256, 256], replicated, may hold values from -0.375 to 0.375
- coarse_bias: float32 [4, 256], replicated, may hold values from -3 to 3
- coarse_gain: float32 [2, 256], replicated, may hold values from 0.1 to 1.9
Outputs:
- fine_out: bfloat16 [65536, 256], P(('group', 'dom'))
- coarse_out: bfloat16 [8192, 256], P(('group', 'dom'))
The draws below stay inside these ranges and needn't reach their ends.
Inputs may be any that keep to these rules, and one draw needn't show every extreme that they name: `edge_send`: indices into the block's extended rows: below 512 the lower neighbour's rows, from 2560 on the upper neighbour's; a block never names the rows of a neighbour it lacks. `cedge_send`: indices into the block's extended coarse rows: below 128 the lower neighbour's rows, from 384 on the upper neighbour's; a block never names the rows of a neighbour it lacks.
All inputs are finite; a program needn't handle non-finite values.
Results may differ from the reference program's by a relative error of at most 0.012.
Values may be sent and summed in bfloat16 or wider, within the bound.
A program may use at most 128 MiB of HBM per device.

```python
import math
import jax
import jax.numpy as jnp
import numpy as np
from jax import lax

H = 256
DEG = 4
NODE_DEV = 2048
EDGE_DEV = 8192
HALO = 512
CDEV = 256
CHALO = 128
CEDGE_DEV = 1024
CLUSTERS_COL = 1024
NODES = 65536
EDGES = 262144
CNODES = 8192
CEDGES = 32768
N_GROUP = 4
N_DOM = 8


def rim_senders(base_key, count_all, per_block, row_count, rim_rows, across_odds):
    blocks = jnp.arange(count_all) // per_block % N_DOM
    key_own, key_side, key_place, key_across = jax.random.split(base_key, 4)
    own_index = rim_rows + jax.random.randint(key_own, (count_all,), 0, row_count)
    which_side = jax.random.randint(key_side, (count_all,), 0, 2)
    which_side = jnp.where(blocks == 0, 1, jnp.where(blocks == N_DOM - 1, 0, which_side))
    rim_place = jax.random.randint(key_place, (count_all,), 0, rim_rows)
    remote = jnp.where(which_side == 0, rim_place, rim_rows + row_count + rim_place)
    across = jax.random.randint(key_across, (count_all,), 0, across_odds) == 0
    return jnp.where(across, remote, own_index).astype(jnp.int32)


def draw_edge_send(key, part):
    return rim_senders(jax.random.fold_in(key, 5), EDGES, EDGE_DEV, NODE_DEV, HALO, 8)


def draw_cedge_send(key, part):
    return rim_senders(jax.random.fold_in(key, 7), CEDGES, CEDGE_DEV, CDEV, CHALO, 2)


def touch_ends(drawn, rng, low, high):
    extent = drawn.shape
    index_at = [jax.random.randint(jax.random.fold_in(rng, axis), (), 0, extent[axis]) for axis in range(len(extent))]
    drawn = drawn.at[tuple(index_at)].set(low)
    longest = extent.index(max(extent))
    index_at[longest] = (index_at[longest] + 1) % extent[longest]
    return drawn.at[tuple(index_at)].set(high)


def steps_of(own_key, dims, cuts, least, high):
    def one(dim, blocks):
        heights = jax.random.uniform(jax.random.fold_in(jax.random.fold_in(own_key, 6), dim), (blocks,), jnp.float32, least / len(cuts), high / len(cuts))
        return jnp.repeat(jnp.exp(heights), dims[dim] // blocks).reshape((-1,) + (1,) * (len(dims) - dim - 1))

    loudness = one(*cuts[0])
    for cut in cuts[1:]:
        loudness = loudness * one(*cut)
    return loudness


def rank_bounds(number_of, skew):
    portions = [(1 << 20) // math.isqrt(rank ** skew) + 1 for rank in range(1, number_of + 1)]
    scale = 1 + sum(portions) // (1 << 30)
    return np.cumsum(np.array([max(1, weight // scale) for weight in portions]))


def ranked_ids(own_key, extent, number_of, skew):
    grid = rank_bounds(number_of, skew)
    ticket = jax.random.randint(jax.random.fold_in(own_key, 1), extent, 0, int(grid[number_of - 1]))
    rank = jnp.searchsorted(jnp.asarray(grid, jnp.int32), ticket, side="right")
    return jax.random.permutation(jax.random.fold_in(own_key, 2), number_of)[rank].astype(jnp.int32)


def gaussian(stream_key, extent, spread, reach, cuts=(), kind=jnp.bfloat16):
    factor_of = steps_of(stream_key, extent, cuts, -0.22, 0.18) if cuts else 1.0
    array = jax.random.normal(stream_key, extent, jnp.float32) * spread * factor_of
    return jnp.minimum(jnp.maximum(array, -reach), reach).astype(kind)


def setup_inputs(seed: int = 0) -> dict:
    arg_keys = jax.random.split(jax.random.key(seed), 22)
    return {
        "node_lat": gaussian(arg_keys[0], (NODES, H), 1.0, 6.0, ((0, 32),)),
        "edge_lat": gaussian(arg_keys[1], (EDGES, H), 1.0, 6.0, ((0, 32),)),
        "edge_send": draw_edge_send(jax.random.fold_in(arg_keys[21], 71), 0),
        "halo_list": touch_ends(jax.random.randint(arg_keys[3], (N_GROUP * N_DOM * 2 * HALO,), 0, NODE_DEV), jax.random.fold_in(arg_keys[3], 1), 0, NODE_DEV - 1).astype(jnp.int32),
        "pool_id": touch_ends(ranked_ids(arg_keys[4], (NODES,), CLUSTERS_COL, 1), jax.random.fold_in(arg_keys[4], 3), 0, CLUSTERS_COL - 1).astype(jnp.int32),
        "coarse_lat": gaussian(arg_keys[5], (CNODES, H), 1.0, 6.0, ((0, 32),)),
        "cedge_lat": gaussian(arg_keys[6], (CEDGES, H), 1.0, 6.0, ((0, 32),)),
        "cedge_send": draw_cedge_send(jax.random.fold_in(arg_keys[21], 71), 0),
        "chalo_list": touch_ends(jax.random.randint(arg_keys[8], (N_GROUP * N_DOM * 2 * CHALO,), 0, CDEV), jax.random.fold_in(arg_keys[8], 1), 0, CDEV - 1).astype(jnp.int32),
        "fine_edge_in": gaussian(arg_keys[9], (3, H, H), (3 * H) ** -0.5, 0.21875),
        "fine_edge_out": gaussian(arg_keys[10], (H, H), H ** -0.5, 0.375),
        "fine_node_in": gaussian(arg_keys[11], (2, H, H), (2 * H) ** -0.5, 0.25),
        "fine_node_out": gaussian(arg_keys[12], (H, H), H ** -0.5, 0.375),
        "fine_bias": gaussian(arg_keys[13], (4, H), 0.5, 3.0, (), jnp.float32),
        "fine_gain": jnp.clip(1.0 + 0.18 * jax.random.normal(arg_keys[14], (2, H), jnp.float32), 0.1, 1.9),
        "coarse_edge_in": gaussian(arg_keys[15], (3, H, H), (3 * H) ** -0.5, 0.21875),
        "coarse_edge_out": gaussian(arg_keys[16], (H, H), H ** -0.5, 0.375),
        "coarse_node_in": gaussian(arg_keys[17], (2, H, H), (2 * H) ** -0.5, 0.25),
        "coarse_node_out": gaussian(arg_keys[18], (H, H), H ** -0.5, 0.375),
        "coarse_bias": gaussian(arg_keys[19], (4, H), 0.5, 3.0, (), jnp.float32),
        "coarse_gain": jnp.clip(1.0 + 0.18 * jax.random.normal(arg_keys[20], (2, H), jnp.float32), 0.1, 1.9),
    }


EPSILON = 1e-05

def layer_norm_rows(values):
    row_mean = lax.optimization_barrier(jnp.mean(values, axis=-1, keepdims=True))
    centred = values - row_mean
    variance = lax.optimization_barrier(jnp.mean(centred * centred, axis=-1, keepdims=True))
    return centred * lax.rsqrt(variance + EPSILON)

def edge_node(sender_proj, own_rows, edge_rows, senders, edge_in, edge_out, node_in, node_out, biases, gains):
    node_count = own_rows.shape[0]
    width = own_rows.shape[1]
    receiver_proj = jnp.dot(own_rows, edge_in[1], preferred_element_type=jnp.float32)
    edge_pre = jnp.dot(edge_rows, edge_in[2], preferred_element_type=jnp.float32)
    edge_pre = edge_pre + sender_proj[senders].astype(jnp.float32) + biases[0]
    edge_pre = (edge_pre.reshape(node_count, DEG, width) + receiver_proj[:, None, :]).reshape(node_count * DEG, width)
    edge_hidden = jnp.maximum(edge_pre, 0.0).astype(jnp.bfloat16)
    message = layer_norm_rows(jnp.dot(edge_hidden, edge_out, preferred_element_type=jnp.float32) + biases[1]) * gains[0]
    message = message.astype(jnp.bfloat16)
    summed = lax.optimization_barrier(jnp.sum(message.astype(jnp.float32).reshape(node_count, DEG, width), axis=1)).astype(jnp.bfloat16)
    node_pre = jnp.dot(own_rows, node_in[0], preferred_element_type=jnp.float32)
    node_pre = node_pre + jnp.dot(summed, node_in[1], preferred_element_type=jnp.float32) + biases[2]
    node_hidden = jnp.maximum(node_pre, 0.0).astype(jnp.bfloat16)
    update = layer_norm_rows(jnp.dot(node_hidden, node_out, preferred_element_type=jnp.float32) + biases[3]) * gains[1]
    return (own_rows.astype(jnp.float32) + update).astype(jnp.bfloat16)

def pick_rows(block_rows, chosen):
    return block_rows[chosen]

def extend_blocks(blocks, lists, rim_rows):
    border = jax.vmap(jax.vmap(pick_rows))(blocks, lists)
    zeros_rim = jnp.zeros_like(border[:, :1, :rim_rows])
    from_lower = jnp.concatenate([zeros_rim, border[:, :-1, rim_rows:]], axis=1)
    from_upper = jnp.concatenate([border[:, 1:, :rim_rows], zeros_rim], axis=1)
    return jnp.concatenate([from_lower, blocks, from_upper], axis=2)

def run_level(node_rows, edge_rows, senders, lists, per_nodes, per_edges, rim_rows, edge_in, edge_out, node_in, node_out, biases, gains):
    block_count = N_GROUP * N_DOM
    width = node_rows.shape[1]
    blocks = node_rows.reshape(N_GROUP, N_DOM, per_nodes, width)
    chosen = lists.reshape(N_GROUP, N_DOM, 2 * rim_rows)
    extended = extend_blocks(blocks, chosen, rim_rows).reshape(block_count, per_nodes + 2 * rim_rows, width)

    def one_block(pieces):
        ext_rows, own_rows, block_edges, send_idx = pieces
        sender_proj = jnp.dot(ext_rows, edge_in[0], preferred_element_type=jnp.float32).astype(jnp.bfloat16)
        return edge_node(sender_proj, own_rows, block_edges, send_idx, edge_in, edge_out, node_in, node_out, biases, gains)
    result = lax.map(one_block, (extended, node_rows.reshape(block_count, per_nodes, width), edge_rows.reshape(block_count, per_edges, width), senders.reshape(block_count, per_edges)))
    return result.reshape(block_count * per_nodes, width)

def reference(node_lat, edge_lat, edge_send, halo_list, pool_id, coarse_lat, cedge_lat, cedge_send, chalo_list, fine_edge_in, fine_edge_out, fine_node_in, fine_node_out, fine_bias, fine_gain, coarse_edge_in, coarse_edge_out, coarse_node_in, coarse_node_out, coarse_bias, coarse_gain):
    block_count = N_GROUP * N_DOM
    fine_out = run_level(node_lat, edge_lat, edge_send, halo_list, NODE_DEV, EDGE_DEV, HALO, fine_edge_in, fine_edge_out, fine_node_in, fine_node_out, fine_bias, fine_gain)

    def block_pool(pieces):
        block_rows, block_ids = pieces
        cluster_sum = jax.ops.segment_sum(block_rows.astype(jnp.float32), block_ids, num_segments=CLUSTERS_COL)
        member_count = jax.ops.segment_sum(jnp.ones(block_ids.shape, jnp.float32), block_ids, num_segments=CLUSTERS_COL)
        return (cluster_sum, member_count)
    partial_sums, partial_counts = lax.map(block_pool, (fine_out.reshape(block_count, NODE_DEV, H), pool_id.reshape(block_count, NODE_DEV)))
    cluster_sum = partial_sums.reshape(N_GROUP, N_DOM, N_GROUP, CDEV, H).sum(axis=0).transpose(1, 0, 2, 3)
    member_count = partial_counts.reshape(N_GROUP, N_DOM, N_GROUP, CDEV).sum(axis=0).transpose(1, 0, 2)
    pooled_mean = cluster_sum / jnp.maximum(member_count, 1.0)[..., None]
    coarse_in = (coarse_lat.astype(jnp.float32) + pooled_mean.reshape(CNODES, H)).astype(jnp.bfloat16)
    coarse_out = run_level(coarse_in, cedge_lat, cedge_send, chalo_list, CDEV, CEDGE_DEV, CHALO, coarse_edge_in, coarse_edge_out, coarse_node_in, coarse_node_out, coarse_bias, coarse_gain)
    return (fine_out, coarse_out)
```

```python
import functools

import jax
import jax.numpy as jnp
from jax import lax
from jax.experimental import pallas as pl
from jax.experimental.pallas import tpu as pltpu
from jax.sharding import PartitionSpec as P

EPSILON = 1e-05
F32 = jnp.float32
BF16 = jnp.bfloat16
NT = 128
DEG = 4


def dot(a, b):
    return jnp.dot(a, b, preferred_element_type=F32)


def centre(weight):
    w = weight.astype(F32)
    return (w - jnp.mean(w, axis=-1, keepdims=True)).astype(BF16)


def unit_rows(z):
    return z * lax.rsqrt(jnp.mean(z * z, axis=-1, keepdims=True) + EPSILON)


def fine_kernel(
    groups, clusters,
    send, pool, node, low, high, edge, ein, eout, nin, nout, bias, gain,
    out, part,
    table, proj, scale, gath, pre_lo, pre_hi, recv, npre, eoc, noc, bc, acc, cnt,
):
    step = pl.program_id(0)
    steps = pl.num_programs(0)
    rows = node.shape[0]
    rim = low.shape[0]
    et = NT * DEG

    def fetch(tile, k, n):
        at = send[tile * et + n * DEG + k]
        gath[pl.ds(k * NT + n, 1), :] = table[pl.ds(at, 1), :]

    @pl.when(step == 0)
    def _():
        eoc[...] = centre(eout[...])
        noc[...] = centre(nout[...])
        b = bias[...]
        bc[...] = b - jnp.mean(b, axis=-1, keepdims=True)
        top = jnp.zeros((1, 256), F32)
        for ref, start in ((low, 0), (node, rim), (high, rim + rows)):
            for r in range(0, ref.shape[0], 256):
                p = dot(ref[r:r + 256, :], ein[0])
                proj[start + r:start + r + 256, :] = p
                top = jnp.maximum(top, jnp.max(jnp.abs(p), axis=0, keepdims=True))
        top = jnp.maximum(top, 1e-20)
        scale[...] = top * (1.0 / 32767.0)
        inv = 32767.0 / top
        for r in range(0, rows + 2 * rim, 256):
            q = jnp.round(proj[r:r + 256, :] * inv).astype(jnp.int32)
            table[r:r + 256, :] = (q[:, :128] & 0xFFFF) | (q[:, 128:] << 16)
        for r in range(0, rows, 256):
            own = node[r:r + 256, :]
            recv[r:r + 256, :] = dot(own, ein[1]) + bias[0:1, :]
            npre[r:r + 256, :] = dot(own, nin[0]) + bias[2:3, :]
        acc[...] = jnp.zeros_like(acc)
        cnt[...] = jnp.zeros_like(cnt)

        def first(n, carry):
            for k in range(DEG):
                fetch(0, k, n)
            return carry

        lax.fori_loop(0, NT, first, 0, unroll=8)

    base = pl.multiple_of(step * NT, NT)
    nxt = jnp.minimum(step + 1, steps - 1)
    p = dot(edge[...], ein[2])
    pre_lo[...] = p[:, :128]
    pre_hi[...] = p[:, 128:]
    rv = recv[pl.ds(base, NT), :]
    total = jnp.zeros((NT, 256), F32)
    for k in range(DEG):
        g = gath[k * NT:(k + 1) * NT, :]
        s = jnp.concatenate([(g << 16) >> 16, g >> 16], axis=1).astype(F32) * scale[...]
        e = jnp.concatenate(
            [pre_lo[pl.ds(k, NT, stride=DEG), :], pre_hi[pl.ds(k, NT, stride=DEG), :]], axis=1
        )
        h = jnp.maximum(e + s + rv, 0.0).astype(BF16)
        total = total + unit_rows(dot(h, eoc[...]) + bc[1:2, :])
        for n in range(NT):
            fetch(nxt, k, n)
    summed = (total * gain[0:1, :]).astype(BF16)
    h = jnp.maximum(npre[pl.ds(base, NT), :] + dot(summed, nin[1]), 0.0).astype(BF16)
    update = unit_rows(dot(h, noc[...]) + bc[3:4, :]) * gain[1:2, :]
    result = (node[pl.ds(base, NT), :].astype(F32) + update).astype(BF16)
    out[...] = result
    ids = pool[pl.ds(step, 1), :]
    ones = jnp.ones((16, NT), BF16)
    for g in range(groups):
        c = g * clusters
        names = lax.broadcasted_iota(jnp.int32, (clusters, NT), 0) + c
        member = jnp.where(names == ids, 1.0, 0.0).astype(BF16)
        acc[c:c + clusters, :] += dot(member, result)
        cnt[g] += lax.dot_general(
            ones, member, (((1,), (1,)), ((), ())), preferred_element_type=F32
        )

    @pl.when(step == steps - 1)
    def _():
        for g in range(groups):
            c = g * clusters
            part[g, 0:clusters, :] = acc[c:c + clusters, :].astype(BF16)
            n = cnt[g]
            big = jnp.floor(n * (1.0 / 256.0)) * 256.0
            which = lax.broadcasted_iota(jnp.int32, n.shape, 0)
            part[g, clusters:clusters + 16, :] = jnp.where(
                which == 0, n - big, jnp.where(which == 1, big, 0.0)
            ).astype(BF16)


def fine_level(groups, clusters, send, pool, node, low, high, edge, ein, eout, nin, nout, bias, gain):
    rows, width = node.shape
    rim = low.shape[0]
    steps = rows // NT
    et = NT * DEG
    whole = pl.BlockSpec(memory_space=pltpu.VMEM)
    return pl.pallas_call(
        functools.partial(fine_kernel, groups, clusters),
        grid=(steps,),
        in_specs=[pl.BlockSpec(memory_space=pltpu.SMEM), whole, whole, whole, whole,
                  pl.BlockSpec((et, width), lambda i: (i, 0))] + [whole] * 6,
        out_specs=[pl.BlockSpec((NT, width), lambda i: (i, 0)),
                   pl.BlockSpec((groups, clusters + 16, width), lambda i: (0, 0, 0))],
        out_shape=[jax.ShapeDtypeStruct((rows, width), BF16),
                   jax.ShapeDtypeStruct((groups, clusters + 16, width), BF16)],
        scratch_shapes=[
            pltpu.VMEM((rows + 2 * rim, 128), jnp.int32),
            pltpu.VMEM((rows + 2 * rim, width), F32),
            pltpu.VMEM((1, width), F32),
            pltpu.VMEM((et, 128), jnp.int32),
            pltpu.VMEM((et, 128), F32),
            pltpu.VMEM((et, 128), F32),
            pltpu.VMEM((rows, width), F32),
            pltpu.VMEM((rows, width), F32),
            pltpu.VMEM((width, width), BF16),
            pltpu.VMEM((width, width), BF16),
            pltpu.VMEM((4, width), F32),
            pltpu.VMEM((groups * clusters, width), F32),
            pltpu.VMEM((groups, 16, clusters), F32),
        ],
        compiler_params=pltpu.CompilerParams(vmem_limit_bytes=48 * 1024 * 1024),
        cost_estimate=pl.CostEstimate(flops=7_000_000_000, bytes_accessed=9_000_000, transcendentals=0),
        name="fine_level",
    )(send, pool.reshape(steps, NT), node, low, high, edge, ein, eout, nin, nout, bias, gain)


def border(rows, chosen):
    table = (chosen[:, None] == jnp.arange(rows.shape[0], dtype=jnp.int32)[None, :]).astype(BF16)
    return dot(table, rows).astype(BF16)


def exchange(edge_rows, rim):
    count = lax.axis_size("dom")
    forward = [(i, i + 1) for i in range(count - 1)]
    backward = [(t, s) for s, t in forward]
    return (lax.ppermute(edge_rows[rim:], "dom", forward),
            lax.ppermute(edge_rows[:rim], "dom", backward))


def layer_norm_rows(values):
    row_mean = jnp.mean(values, axis=-1, keepdims=True)
    centred = values - row_mean
    variance = jnp.mean(centred * centred, axis=-1, keepdims=True)
    return centred * lax.rsqrt(variance + EPSILON)


def edge_node(
    sender_proj, own_rows, edge_rows, senders, edge_in, edge_out, node_in, node_out, biases, gains
):
    node_count = own_rows.shape[0]
    width = own_rows.shape[1]
    fanin = edge_rows.shape[0] // node_count
    receiver_proj = dot(own_rows, edge_in[1])
    edge_pre = dot(edge_rows, edge_in[2])
    edge_pre = edge_pre + sender_proj[senders].astype(F32) + biases[0]
    edge_pre = (edge_pre.reshape(node_count, fanin, width) + receiver_proj[:, None, :]).reshape(
        node_count * fanin, width
    )
    edge_hidden = jnp.maximum(edge_pre, 0.0).astype(BF16)
    message = layer_norm_rows(dot(edge_hidden, edge_out) + biases[1]) * gains[0]
    message = message.astype(BF16)
    summed = jnp.sum(message.astype(F32).reshape(node_count, fanin, width), axis=1).astype(BF16)
    node_pre = dot(own_rows, node_in[0]) + dot(summed, node_in[1]) + biases[2]
    node_hidden = jnp.maximum(node_pre, 0.0).astype(BF16)
    update = layer_norm_rows(dot(node_hidden, node_out) + biases[3]) * gains[1]
    return (own_rows.astype(F32) + update).astype(BF16)


def body(
    node_lat, edge_lat, edge_send, halo_list, pool_id,
    coarse_lat, cedge_lat, cedge_send, chalo_list,
    fine_edge_in, fine_edge_out, fine_node_in, fine_node_out, fine_bias, fine_gain,
    coarse_edge_in, coarse_edge_out, coarse_node_in, coarse_node_out, coarse_bias, coarse_gain,
):
    groups = lax.axis_size("group")
    clusters, width = coarse_lat.shape
    rim = halo_list.shape[0] // 2
    low, high = exchange(border(node_lat, halo_list), rim)
    fine_out, part = fine_level(
        groups, clusters, edge_send, pool_id, node_lat, low, high, edge_lat,
        fine_edge_in, fine_edge_out, fine_node_in, fine_node_out, fine_bias, fine_gain,
    )
    got = lax.all_to_all(part, "group", split_axis=0, concat_axis=0, tiled=True).astype(F32)
    got = got.sum(axis=0)
    cluster_sum = got[:clusters]
    member_count = got[clusters] + got[clusters + 1]
    pooled_mean = cluster_sum / jnp.maximum(member_count, 1.0)[:, None]
    coarse_in = (coarse_lat.astype(F32) + pooled_mean).astype(BF16)
    crim = chalo_list.shape[0] // 2
    clow, chigh = exchange(border(coarse_in, chalo_list), crim)
    cext = jnp.concatenate([clow, coarse_in, chigh], axis=0)
    coarse_out = edge_node(
        dot(cext, coarse_edge_in[0]).astype(BF16),
        coarse_in, cedge_lat, cedge_send,
        coarse_edge_in, coarse_edge_out, coarse_node_in, coarse_node_out, coarse_bias, coarse_gain,
    )
    return (fine_out, coarse_out)


def solution(mesh):
    both = ("group", "dom")
    rows, flat = P(both, None), P(both)
    placed = (rows, rows, flat, flat, flat, rows, rows, flat, flat) + (P(),) * 12
    return jax.shard_map(body, mesh=mesh, in_specs=placed, out_specs=(rows, rows), check_vma=False)
```

```python
import functools

import jax
import jax.numpy as jnp
from jax import lax
from jax.experimental import pallas as pl
from jax.experimental.pallas import tpu as pltpu
from jax.sharding import PartitionSpec as P

EPSILON = 1e-05
F32 = jnp.float32
BF16 = jnp.bfloat16
NT = 128
DEG = 4


def dot(a, b):
    return jnp.dot(a, b, preferred_element_type=F32)


def centre(weight):
    w = weight.astype(F32)
    return (w - jnp.mean(w, axis=-1, keepdims=True)).astype(BF16)


def unit_rows(z):
    return z * lax.rsqrt(jnp.mean(z * z, axis=-1, keepdims=True) + EPSILON)


def fine_kernel(
    groups, clusters,
    send, pool, node, low, high, edge, ein, eout, nin, nout, bias, gain,
    out, part,
    table, proj, scale, gath, pre_lo, pre_hi, recv, npre, eoc, noc, bc, acc, cnt,
):
    step = pl.program_id(0)
    steps = pl.num_programs(0)
    rows = node.shape[0]
    rim = low.shape[0]
    et = NT * DEG

    def fetch(tile, k, n):
        at = send[tile * et + n * DEG + k]
        gath[pl.ds(k * NT + n, 1), :] = table[pl.ds(at, 1), :]

    @pl.when(step == 0)
    def _():
        eoc[...] = centre(eout[...])
        noc[...] = centre(nout[...])
        b = bias[...]
        bc[...] = b - jnp.mean(b, axis=-1, keepdims=True)
        top = jnp.zeros((1, 256), F32)
        for ref, start in ((low, 0), (node, rim), (high, rim + rows)):
            for r in range(0, ref.shape[0], 256):
                p = dot(ref[r:r + 256, :], ein[0])
                proj[start + r:start + r + 256, :] = p
                top = jnp.maximum(top, jnp.max(jnp.abs(p), axis=0, keepdims=True))
        top = jnp.maximum(top, 1e-20)
        scale[...] = top * (1.0 / 32767.0)
        inv = 32767.0 / top
        for r in range(0, rows + 2 * rim, 256):
            q = jnp.round(proj[r:r + 256, :] * inv).astype(jnp.int32)
            table[r:r + 256, :] = (q[:, :128] & 0xFFFF) | (q[:, 128:] << 16)
        for r in range(0, rows, 256):
            own = node[r:r + 256, :]
            recv[r:r + 256, :] = dot(own, ein[1]) + bias[0:1, :]
            npre[r:r + 256, :] = dot(own, nin[0]) + bias[2:3, :]
        acc[...] = jnp.zeros_like(acc)
        cnt[...] = jnp.zeros_like(cnt)

        def first(n, carry):
            for k in range(DEG):
                fetch(0, k, n)
            return carry

        lax.fori_loop(0, NT, first, 0, unroll=8)

    base = pl.multiple_of(step * NT, NT)
    nxt = jnp.minimum(step + 1, steps - 1)
    p = dot(edge[...], ein[2])
    pre_lo[...] = p[:, :128]
    pre_hi[...] = p[:, 128:]
    rv = recv[pl.ds(base, NT), :]
    total = jnp.zeros((NT, 256), F32)
    for k in range(DEG):
        g = gath[k * NT:(k + 1) * NT, :]
        s = jnp.concatenate([(g << 16) >> 16, g >> 16], axis=1).astype(F32) * scale[...]
        e = jnp.concatenate(
            [pre_lo[pl.ds(k, NT, stride=DEG), :], pre_hi[pl.ds(k, NT, stride=DEG), :]], axis=1
        )
        h = jnp.maximum(e + s + rv, 0.0).astype(BF16)
        total = total + unit_rows(dot(h, eoc[...]) + bc[1:2, :])
        for n in range(NT):
            fetch(nxt, k, n)
    summed = (total * gain[0:1, :]).astype(BF16)
    h = jnp.maximum(npre[pl.ds(base, NT), :] + dot(summed, nin[1]), 0.0).astype(BF16)
    update = unit_rows(dot(h, noc[...]) + bc[3:4, :]) * gain[1:2, :]
    result = (node[pl.ds(base, NT), :].astype(F32) + update).astype(BF16)
    out[...] = result
    ids = pool[pl.ds(step, 1), :]
    ones = jnp.ones((16, NT), BF16)
    for g in range(groups):
        c = g * clusters
        names = lax.broadcasted_iota(jnp.int32, (clusters, NT), 0) + c
        member = jnp.where(names == ids, 1.0, 0.0).astype(BF16)
        acc[c:c + clusters, :] += dot(member, result)
        cnt[g] += lax.dot_general(
            ones, member, (((1,), (1,)), ((), ())), preferred_element_type=F32
        )

    @pl.when(step == steps - 1)
    def _():
        for g in range(groups):
            c = g * clusters
            part[g, 0:clusters, :] = acc[c:c + clusters, :].astype(BF16)
            n = cnt[g]
            big = jnp.floor(n * (1.0 / 256.0)) * 256.0
            which = lax.broadcasted_iota(jnp.int32, n.shape, 0)
            part[g, clusters:clusters + 16, :] = jnp.where(
                which == 0, n - big, jnp.where(which == 1, big, 0.0)
            ).astype(BF16)


def fine_level(groups, clusters, send, pool, node, low, high, edge, ein, eout, nin, nout, bias, gain):
    rows, width = node.shape
    rim = low.shape[0]
    steps = rows // NT
    et = NT * DEG
    whole = pl.BlockSpec(memory_space=pltpu.VMEM)
    return pl.pallas_call(
        functools.partial(fine_kernel, groups, clusters),
        grid=(steps,),
        in_specs=[pl.BlockSpec(memory_space=pltpu.SMEM), whole, whole, whole, whole,
                  pl.BlockSpec((et, width), lambda i: (i, 0))] + [whole] * 6,
        out_specs=[pl.BlockSpec((NT, width), lambda i: (i, 0)),
                   pl.BlockSpec((groups, clusters + 16, width), lambda i: (0, 0, 0))],
        out_shape=[jax.ShapeDtypeStruct((rows, width), BF16),
                   jax.ShapeDtypeStruct((groups, clusters + 16, width), BF16)],
        scratch_shapes=[
            pltpu.VMEM((rows + 2 * rim, 128), jnp.int32),
            pltpu.VMEM((rows + 2 * rim, width), F32),
            pltpu.VMEM((1, width), F32),
            pltpu.VMEM((et, 128), jnp.int32),
            pltpu.VMEM((et, 128), F32),
            pltpu.VMEM((et, 128), F32),
            pltpu.VMEM((rows, width), F32),
            pltpu.VMEM((rows, width), F32),
            pltpu.VMEM((width, width), BF16),
            pltpu.VMEM((width, width), BF16),
            pltpu.VMEM((4, width), F32),
            pltpu.VMEM((groups * clusters, width), F32),
            pltpu.VMEM((groups, 16, clusters), F32),
        ],
        compiler_params=pltpu.CompilerParams(vmem_limit_bytes=48 * 1024 * 1024),
        cost_estimate=pl.CostEstimate(flops=7_000_000_000, bytes_accessed=9_000_000, transcendentals=0),
        name="fine_level",
    )(send, pool.reshape(steps, NT), node, low, high, edge, ein, eout, nin, nout, bias, gain)


def border(rows, chosen):
    table = (chosen[:, None] == jnp.arange(rows.shape[0], dtype=jnp.int32)[None, :]).astype(BF16)
    return dot(table, rows).astype(BF16)


def exchange(edge_rows, rim):
    count = lax.axis_size("dom")
    forward = [(i, i + 1) for i in range(count - 1)]
    backward = [(t, s) for s, t in forward]
    return (lax.ppermute(edge_rows[rim:], "dom", forward),
            lax.ppermute(edge_rows[:rim], "dom", backward))


def coarse_kernel(
    part, lat, edge, sends, lists, ein, eout, nin, nout, bias, gain,
    out,
    got, edges_lo, edges_hi, rim_out, rim_in, mix, sum_send, sum_recv, rim_send, rim_recv,
):
    groups = part.shape[0]
    rows, width = lat.shape
    rim = rim_in.shape[1]
    mine = lax.axis_index("group")
    here = lax.axis_index("dom")
    last = lax.axis_size("dom") - 1
    has_low = here > 0
    has_high = here < last
    below = jnp.maximum(here - 1, 0)
    above = jnp.minimum(here + 1, last)
    mesh_id = pl.DeviceIdType.MESH

    barrier = pltpu.get_barrier_semaphore()
    for o in range(1, groups):
        pl.semaphore_signal(
            barrier, inc=1, device_id=(lax.rem(mine + o, groups), here), device_id_type=mesh_id
        )

    @pl.when(has_low)
    def _():
        pl.semaphore_signal(barrier, inc=1, device_id=(mine, below), device_id_type=mesh_id)

    @pl.when(has_high)
    def _():
        pl.semaphore_signal(barrier, inc=1, device_id=(mine, above), device_id_type=mesh_id)

    pl.semaphore_wait(barrier, groups - 1 + has_low.astype(jnp.int32) + has_high.astype(jnp.int32))
    copies = []
    for o in range(1, groups):
        peer = lax.rem(mine + o, groups)
        copy = pltpu.make_async_remote_copy(
            src_ref=part.at[peer], dst_ref=got.at[o - 1],
            send_sem=sum_send.at[o - 1], recv_sem=sum_recv.at[o - 1],
            device_id=(peer, here), device_id_type=mesh_id,
        )
        copy.start()
        copies.append(copy)

    eoc = centre(eout[...])
    noc = centre(nout[...])
    b = bias[...]
    bc = b - jnp.mean(b, axis=-1, keepdims=True)
    for r in range(0, edge.shape[0], 256):
        p = dot(edge[r:r + 256, :], ein[2])
        edges_lo[r:r + 256, :] = p[:, :128]
        edges_hi[r:r + 256, :] = p[:, 128:]
    sums = part[mine].astype(F32)
    for copy in copies:
        copy.wait_recv()
    for o in range(1, groups):
        sums = sums + got[o - 1].astype(F32)
    members = sums[rows:rows + 1, :] + sums[rows + 1:rows + 2, :]
    inv = jnp.broadcast_to(1.0 / jnp.maximum(members, 1.0), (128, rows)).T
    inv = jnp.concatenate([inv] * (width // 128), axis=1)
    own = (lat[...].astype(F32) + sums[:rows, :] * inv).astype(BF16)
    names = lax.broadcasted_iota(jnp.int32, (2 * rim, rows), 1)
    chosen = jnp.where(names == lists[...], 1.0, 0.0).astype(BF16)
    border_rows = dot(chosen, own).astype(BF16)
    rim_out[0] = border_rows[:rim, :]
    rim_out[1] = border_rows[rim:, :]
    down = pltpu.make_async_remote_copy(
        src_ref=rim_out.at[0], dst_ref=rim_in.at[1],
        send_sem=rim_send.at[0], recv_sem=rim_recv.at[0],
        device_id=(mine, below), device_id_type=mesh_id,
    )
    up = pltpu.make_async_remote_copy(
        src_ref=rim_out.at[1], dst_ref=rim_in.at[0],
        send_sem=rim_send.at[1], recv_sem=rim_recv.at[1],
        device_id=(mine, above), device_id_type=mesh_id,
    )

    @pl.when(has_low)
    def _():
        down.start()

    @pl.when(has_high)
    def _():
        up.start()

    @pl.when(jnp.logical_not(has_low))
    def _():
        rim_in[0] = jnp.zeros((rim, width), BF16)

    @pl.when(jnp.logical_not(has_high))
    def _():
        rim_in[1] = jnp.zeros((rim, width), BF16)

    sender = dot(own, ein[0]).astype(BF16)
    recv = dot(own, ein[1]) + b[0:1, :]
    npre = dot(own, nin[0]) + b[2:3, :]
    inner = lax.broadcasted_iota(jnp.int32, (rows, rows), 1) + rim
    outer = lax.broadcasted_iota(jnp.int32, (rows, 2 * rim), 1)
    outer = outer + jnp.where(outer >= rim, rows, 0)
    for k in range(DEG):
        member = jnp.where(inner == sends[:, k:k + 1], 1.0, 0.0).astype(BF16)
        e = jnp.concatenate(
            [edges_lo[pl.ds(k, rows, stride=DEG), :], edges_hi[pl.ds(k, rows, stride=DEG), :]],
            axis=1,
        )
        mix[k] = e + recv + dot(member, sender)

    @pl.when(has_high)
    def _():
        down.wait_recv()

    @pl.when(has_low)
    def _():
        up.wait_recv()

    low = dot(rim_in[0], ein[0]).astype(BF16)
    high = dot(rim_in[1], ein[0]).astype(BF16)
    rims = jnp.concatenate([low, high], axis=0)
    total = jnp.zeros((rows, width), F32)
    for k in range(DEG):
        member = jnp.where(outer == sends[:, k:k + 1], 1.0, 0.0).astype(BF16)
        h = jnp.maximum(mix[k] + dot(member, rims), 0.0).astype(BF16)
        total = total + unit_rows(dot(h, eoc) + bc[1:2, :])
    summed = (total * gain[0:1, :]).astype(BF16)
    h = jnp.maximum(npre + dot(summed, nin[1]), 0.0).astype(BF16)
    update = unit_rows(dot(h, noc) + bc[3:4, :]) * gain[1:2, :]
    out[...] = (own.astype(F32) + update).astype(BF16)
    for copy in copies:
        copy.wait_send()

    @pl.when(has_low)
    def _():
        down.wait_send()

    @pl.when(has_high)
    def _():
        up.wait_send()


def coarse_level(part, lat, edge, send, lists, ein, eout, nin, nout, bias, gain):
    groups = part.shape[0]
    rows, width = lat.shape
    rim = lists.shape[0] // 2
    return pl.pallas_call(
        coarse_kernel,
        in_specs=[pl.BlockSpec(memory_space=pltpu.VMEM)] * 11,
        out_specs=pl.BlockSpec(memory_space=pltpu.VMEM),
        out_shape=jax.ShapeDtypeStruct((rows, width), BF16),
        scratch_shapes=[
            pltpu.VMEM((groups - 1,) + part.shape[1:], BF16),
            pltpu.VMEM((edge.shape[0], 128), F32),
            pltpu.VMEM((edge.shape[0], 128), F32),
            pltpu.VMEM((2, rim, width), BF16),
            pltpu.VMEM((2, rim, width), BF16),
            pltpu.VMEM((DEG, rows, width), F32),
            pltpu.SemaphoreType.DMA((groups - 1,)),
            pltpu.SemaphoreType.DMA((groups - 1,)),
            pltpu.SemaphoreType.DMA((2,)),
            pltpu.SemaphoreType.DMA((2,)),
        ],
        compiler_params=pltpu.CompilerParams(
            vmem_limit_bytes=32 * 1024 * 1024, collective_id=0, has_side_effects=True
        ),
        cost_estimate=pl.CostEstimate(flops=1_500_000_000, bytes_accessed=3_000_000, transcendentals=0),
        name="coarse_level",
    )(part, lat, edge, send.reshape(rows, DEG), lists.reshape(2 * rim, 1),
      ein, eout, nin, nout, bias, gain)


def body(
    node_lat, edge_lat, edge_send, halo_list, pool_id,
    coarse_lat, cedge_lat, cedge_send, chalo_list,
    fine_edge_in, fine_edge_out, fine_node_in, fine_node_out, fine_bias, fine_gain,
    coarse_edge_in, coarse_edge_out, coarse_node_in, coarse_node_out, coarse_bias, coarse_gain,
):
    groups = lax.axis_size("group")
    clusters, width = coarse_lat.shape
    rim = halo_list.shape[0] // 2
    low, high = exchange(border(node_lat, halo_list), rim)
    fine_out, part = fine_level(
        groups, clusters, edge_send, pool_id, node_lat, low, high, edge_lat,
        fine_edge_in, fine_edge_out, fine_node_in, fine_node_out, fine_bias, fine_gain,
    )
    coarse_out = coarse_level(
        part, coarse_lat, cedge_lat, cedge_send, chalo_list,
        coarse_edge_in, coarse_edge_out, coarse_node_in, coarse_node_out, coarse_bias, coarse_gain,
    )
    return (fine_out, coarse_out)


def solution(mesh):
    both = ("group", "dom")
    rows, flat = P(both, None), P(both)
    placed = (rows, rows, flat, flat, flat, rows, rows, flat, flat) + (P(),) * 12
    return jax.shard_map(body, mesh=mesh, in_specs=placed, out_specs=(rows, rows), check_vma=False)
```

```python
import functools

import jax
import jax.numpy as jnp
from jax import lax
from jax.experimental import pallas as pl
from jax.experimental.pallas import tpu as pltpu
from jax.sharding import PartitionSpec as P

EPSILON = 1e-05
F32 = jnp.float32
BF16 = jnp.bfloat16
NT = 256
DEG = 4


def dot(a, b):
    return jnp.dot(a, b, preferred_element_type=F32)


def centre(weight):
    w = weight.astype(F32)
    return (w - jnp.mean(w, axis=-1, keepdims=True)).astype(BF16)


def unit_rows(z):
    return z * lax.rsqrt(jnp.mean(z * z, axis=-1, keepdims=True) + EPSILON)


def column(row):
    return jnp.broadcast_to(row, (128, 128)).T


def neighbours():
    here = lax.axis_index("dom")
    last = lax.axis_size("dom") - 1
    return here > 0, here < last, jnp.maximum(here - 1, 0), jnp.minimum(here + 1, last)


def rim_copies(rim_out, rim_in, rim_send, rim_recv, below, above):
    mine = lax.axis_index("group")
    return tuple(
        pltpu.make_async_remote_copy(
            src_ref=rim_out.at[i], dst_ref=rim_in.at[1 - i],
            send_sem=rim_send.at[i], recv_sem=rim_recv.at[i],
            device_id=(mine, to), device_id_type=pl.DeviceIdType.MESH,
        )
        for i, to in enumerate((below, above))
    )


def front_kernel(
    lists, node, ein, table, scale, proj, rim_out, rim_in, rim_send, rim_recv
):
    rows, width = node.shape
    rim = rim_in.shape[1]
    mine = lax.axis_index("group")
    has_low, has_high, below, above = neighbours()
    barrier = pltpu.get_barrier_semaphore()

    @pl.when(has_low)
    def _():
        pl.semaphore_signal(
            barrier, inc=1, device_id=(mine, below), device_id_type=pl.DeviceIdType.MESH
        )

    @pl.when(has_high)
    def _():
        pl.semaphore_signal(
            barrier, inc=1, device_id=(mine, above), device_id_type=pl.DeviceIdType.MESH
        )

    @pl.when(jnp.logical_not(has_low))
    def _():
        rim_in[0] = jnp.zeros((rim, width), BF16)

    @pl.when(jnp.logical_not(has_high))
    def _():
        rim_in[1] = jnp.zeros((rim, width), BF16)

    down, up = rim_copies(rim_out, rim_in, rim_send, rim_recv, below, above)
    lane = lax.broadcasted_iota(jnp.int32, (128, 128), 1)

    def pick(side):
        for r in range(0, rim, 128):
            at = (side * rim + r) // 128
            names = column(lists[at:at + 1, :])
            chosen = jnp.concatenate(
                [jnp.where(names == lane + j, 1.0, 0.0).astype(BF16) for j in range(0, rows, 128)],
                axis=1,
            )
            rim_out[side, r:r + 128, :] = dot(chosen, node[...]).astype(BF16)

    pick(0)
    pl.semaphore_wait(barrier, has_low.astype(jnp.int32) + has_high.astype(jnp.int32))

    @pl.when(has_low)
    def _():
        down.start()

    pick(1)

    @pl.when(has_high)
    def _():
        up.start()

    top = jnp.full((1, width), 1e-20, F32)
    for r in range(0, rows, 256):
        p = dot(node[r:r + 256, :], ein[0])
        proj[rim + r:rim + r + 256, :] = p
        top = jnp.maximum(top, jnp.max(jnp.abs(p), axis=0, keepdims=True))

    @pl.when(has_high)
    def _():
        down.wait_recv()

    @pl.when(has_low)
    def _():
        up.wait_recv()

    for side, start in ((0, 0), (1, rim + rows)):
        for r in range(0, rim, 256):
            p = dot(rim_in[side, r:r + 256, :], ein[0])
            proj[start + r:start + r + 256, :] = p
            top = jnp.maximum(top, jnp.max(jnp.abs(p), axis=0, keepdims=True))
    scale[...] = top * (1.0 / 32767.0)
    inv = 32767.0 / top
    for r in range(0, rows + 2 * rim, 256):
        q = jnp.round(proj[r:r + 256, :] * inv).astype(jnp.int32)
        table[r:r + 256, :] = (q[:, :128] & 0xFFFF) | (q[:, 128:] << 16)

    @pl.when(has_low)
    def _():
        down.wait_send()

    @pl.when(has_high)
    def _():
        up.wait_send()


def front(lists, node, ein):
    rows, width = node.shape
    rim = lists.shape[0] // 2
    return pl.pallas_call(
        front_kernel,
        in_specs=[pl.BlockSpec(memory_space=pltpu.VMEM)] * 3,
        out_specs=[pl.BlockSpec(memory_space=pltpu.VMEM)] * 2,
        out_shape=[jax.ShapeDtypeStruct((rows + 2 * rim, 128), jnp.int32),
                   jax.ShapeDtypeStruct((1, width), F32)],
        scratch_shapes=[
            pltpu.VMEM((rows + 2 * rim, width), F32),
            pltpu.VMEM((2, rim, width), BF16),
            pltpu.VMEM((2, rim, width), BF16),
            pltpu.SemaphoreType.DMA((2,)),
            pltpu.SemaphoreType.DMA((2,)),
        ],
        compiler_params=pltpu.CompilerParams(
            vmem_limit_bytes=32 * 1024 * 1024, collective_id=1, has_side_effects=True
        ),
        cost_estimate=pl.CostEstimate(flops=1_500_000_000, bytes_accessed=3_000_000, transcendentals=0),
        name="front",
    )(lists.reshape(2 * rim // 128, 128), node, ein)


def fine_kernel(
    groups, clusters,
    send, pool, table, scale, node, edge, ein, eout, nin, nout, bias, gain,
    out, part,
    gath, pre_lo, pre_hi, eoc, noc, bc, acc, cnt,
):
    step = pl.program_id(0)
    steps = pl.num_programs(0)
    et = NT * DEG

    def fetch(tile, k, n):
        at = send[tile * et + n * DEG + k]
        gath[pl.ds(k * NT + n, 1), :] = table[at]

    @pl.when(step == 0)
    def _():
        eoc[...] = centre(eout[...])
        noc[...] = centre(nout[...])
        b = bias[...]
        bc[...] = b - jnp.mean(b, axis=-1, keepdims=True)
        acc[...] = jnp.zeros_like(acc)
        cnt[...] = jnp.zeros_like(cnt)

        def first(n, carry):
            for k in range(DEG):
                fetch(0, k, n)
            return carry

        lax.fori_loop(0, NT, first, 0, unroll=8)

    nxt = jnp.minimum(step + 1, steps - 1)
    p = dot(edge[...], ein[2])
    pre_lo[...] = p[:, :128]
    pre_hi[...] = p[:, 128:]
    own = node[...]
    rv = dot(own, ein[1]) + bias[0:1, :]
    total = jnp.zeros((NT, 256), F32)
    for k in range(DEG):
        g = gath[k * NT:(k + 1) * NT, :]
        s = jnp.concatenate([(g << 16) >> 16, g >> 16], axis=1).astype(F32) * scale[...]
        e = jnp.concatenate(
            [pre_lo[pl.ds(k, NT, stride=DEG), :], pre_hi[pl.ds(k, NT, stride=DEG), :]], axis=1
        )
        h = jnp.maximum(e + s + rv, 0.0).astype(BF16)
        total = total + unit_rows(dot(h, eoc[...]) + bc[1:2, :])
        for n in range(NT):
            fetch(nxt, k, n)
    summed = (total * gain[0:1, :]).astype(BF16)
    h = jnp.maximum(dot(own, nin[0]) + dot(summed, nin[1]) + bias[2:3, :], 0.0).astype(BF16)
    update = unit_rows(dot(h, noc[...]) + bc[3:4, :]) * gain[1:2, :]
    result = (own.astype(F32) + update).astype(BF16)
    out[...] = result
    ids = pool[pl.ds(step, 1), :]
    ones = jnp.ones((16, NT), BF16)
    for g in range(groups):
        c = g * clusters
        names = lax.broadcasted_iota(jnp.int32, (clusters, NT), 0) + c
        member = jnp.where(names == ids, 1.0, 0.0).astype(BF16)
        acc[c:c + clusters, :] += dot(member, result)
        cnt[g] += lax.dot_general(
            ones, member, (((1,), (1,)), ((), ())), preferred_element_type=F32
        )

    @pl.when(step == steps - 1)
    def _():
        for g in range(groups):
            c = g * clusters
            part[g, 0:clusters, :] = acc[c:c + clusters, :].astype(BF16)
            n = cnt[g]
            big = jnp.floor(n * (1.0 / 256.0)) * 256.0
            which = lax.broadcasted_iota(jnp.int32, n.shape, 0)
            part[g, clusters:clusters + 16, :] = jnp.where(
                which == 0, n - big, jnp.where(which == 1, big, 0.0)
            ).astype(BF16)


def fine_level(groups, clusters, send, pool, table, scale, node, edge, ein, eout, nin, nout, bias, gain):
    rows, width = node.shape
    steps = rows // NT
    et = NT * DEG
    whole = pl.BlockSpec(memory_space=pltpu.VMEM)
    return pl.pallas_call(
        functools.partial(fine_kernel, groups, clusters),
        grid=(steps,),
        in_specs=[pl.BlockSpec(memory_space=pltpu.SMEM), whole, whole, whole,
                  pl.BlockSpec((NT, width), lambda i: (i, 0)),
                  pl.BlockSpec((et, width), lambda i: (i, 0))] + [whole] * 6,
        out_specs=[pl.BlockSpec((NT, width), lambda i: (i, 0)),
                   pl.BlockSpec((groups, clusters + 16, width), lambda i: (0, 0, 0))],
        out_shape=[jax.ShapeDtypeStruct((rows, width), BF16),
                   jax.ShapeDtypeStruct((groups, clusters + 16, width), BF16)],
        scratch_shapes=[
            pltpu.VMEM((et, 128), jnp.int32),
            pltpu.VMEM((et, 128), F32),
            pltpu.VMEM((et, 128), F32),
            pltpu.VMEM((width, width), BF16),
            pltpu.VMEM((width, width), BF16),
            pltpu.VMEM((4, width), F32),
            pltpu.VMEM((groups * clusters, width), F32),
            pltpu.VMEM((groups, 16, clusters), F32),
        ],
        compiler_params=pltpu.CompilerParams(vmem_limit_bytes=48 * 1024 * 1024),
        cost_estimate=pl.CostEstimate(flops=7_000_000_000, bytes_accessed=9_000_000, transcendentals=0),
        name="fine_level",
    )(send, pool.reshape(steps, NT), table, scale, node, edge, ein, eout, nin, nout, bias, gain)


def coarse_kernel(
    part, lat, edge, sends, lists, ein, eout, nin, nout, bias, gain,
    out,
    got, edges_lo, edges_hi, rim_out, rim_in, mix, sum_send, sum_recv, rim_send, rim_recv,
):
    groups = part.shape[0]
    rows, width = lat.shape
    rim = rim_in.shape[1]
    mine = lax.axis_index("group")
    here = lax.axis_index("dom")
    last = lax.axis_size("dom") - 1
    has_low = here > 0
    has_high = here < last
    below = jnp.maximum(here - 1, 0)
    above = jnp.minimum(here + 1, last)
    mesh_id = pl.DeviceIdType.MESH

    barrier = pltpu.get_barrier_semaphore()
    for o in range(1, groups):
        pl.semaphore_signal(
            barrier, inc=1, device_id=(lax.rem(mine + o, groups), here), device_id_type=mesh_id
        )

    @pl.when(has_low)
    def _():
        pl.semaphore_signal(barrier, inc=1, device_id=(mine, below), device_id_type=mesh_id)

    @pl.when(has_high)
    def _():
        pl.semaphore_signal(barrier, inc=1, device_id=(mine, above), device_id_type=mesh_id)

    pl.semaphore_wait(barrier, groups - 1 + has_low.astype(jnp.int32) + has_high.astype(jnp.int32))
    copies = []
    for o in range(1, groups):
        peer = lax.rem(mine + o, groups)
        copy = pltpu.make_async_remote_copy(
            src_ref=part.at[peer], dst_ref=got.at[o - 1],
            send_sem=sum_send.at[o - 1], recv_sem=sum_recv.at[o - 1],
            device_id=(peer, here), device_id_type=mesh_id,
        )
        copy.start()
        copies.append(copy)

    eoc = centre(eout[...])
    noc = centre(nout[...])
    b = bias[...]
    bc = b - jnp.mean(b, axis=-1, keepdims=True)
    for r in range(0, edge.shape[0], 256):
        p = dot(edge[r:r + 256, :], ein[2])
        edges_lo[r:r + 256, :] = p[:, :128]
        edges_hi[r:r + 256, :] = p[:, 128:]
    sums = part[mine].astype(F32)
    for copy in copies:
        copy.wait_recv()
    for o in range(1, groups):
        sums = sums + got[o - 1].astype(F32)
    members = sums[rows:rows + 1, :] + sums[rows + 1:rows + 2, :]
    inv = jnp.broadcast_to(1.0 / jnp.maximum(members, 1.0), (128, rows)).T
    inv = jnp.concatenate([inv] * (width // 128), axis=1)
    own = (lat[...].astype(F32) + sums[:rows, :] * inv).astype(BF16)
    names = lax.broadcasted_iota(jnp.int32, (2 * rim, rows), 1)
    chosen = jnp.where(names == lists[...], 1.0, 0.0).astype(BF16)
    border_rows = dot(chosen, own).astype(BF16)
    rim_out[0] = border_rows[:rim, :]
    rim_out[1] = border_rows[rim:, :]
    down = pltpu.make_async_remote_copy(
        src_ref=rim_out.at[0], dst_ref=rim_in.at[1],
        send_sem=rim_send.at[0], recv_sem=rim_recv.at[0],
        device_id=(mine, below), device_id_type=mesh_id,
    )
    up = pltpu.make_async_remote_copy(
        src_ref=rim_out.at[1], dst_ref=rim_in.at[0],
        send_sem=rim_send.at[1], recv_sem=rim_recv.at[1],
        device_id=(mine, above), device_id_type=mesh_id,
    )

    @pl.when(has_low)
    def _():
        down.start()

    @pl.when(has_high)
    def _():
        up.start()

    @pl.when(jnp.logical_not(has_low))
    def _():
        rim_in[0] = jnp.zeros((rim, width), BF16)

    @pl.when(jnp.logical_not(has_high))
    def _():
        rim_in[1] = jnp.zeros((rim, width), BF16)

    sender = dot(own, ein[0]).astype(BF16)
    recv = dot(own, ein[1]) + b[0:1, :]
    npre = dot(own, nin[0]) + b[2:3, :]
    inner = lax.broadcasted_iota(jnp.int32, (rows, rows), 1) + rim
    outer = lax.broadcasted_iota(jnp.int32, (rows, 2 * rim), 1)
    outer = outer + jnp.where(outer >= rim, rows, 0)
    for k in range(DEG):
        member = jnp.where(inner == sends[:, k:k + 1], 1.0, 0.0).astype(BF16)
        e = jnp.concatenate(
            [edges_lo[pl.ds(k, rows, stride=DEG), :], edges_hi[pl.ds(k, rows, stride=DEG), :]],
            axis=1,
        )
        mix[k] = e + recv + dot(member, sender)

    @pl.when(has_high)
    def _():
        down.wait_recv()

    @pl.when(has_low)
    def _():
        up.wait_recv()

    low = dot(rim_in[0], ein[0]).astype(BF16)
    high = dot(rim_in[1], ein[0]).astype(BF16)
    rims = jnp.concatenate([low, high], axis=0)
    total = jnp.zeros((rows, width), F32)
    for k in range(DEG):
        member = jnp.where(outer == sends[:, k:k + 1], 1.0, 0.0).astype(BF16)
        h = jnp.maximum(mix[k] + dot(member, rims), 0.0).astype(BF16)
        total = total + unit_rows(dot(h, eoc) + bc[1:2, :])
    summed = (total * gain[0:1, :]).astype(BF16)
    h = jnp.maximum(npre + dot(summed, nin[1]), 0.0).astype(BF16)
    update = unit_rows(dot(h, noc) + bc[3:4, :]) * gain[1:2, :]
    out[...] = (own.astype(F32) + update).astype(BF16)
    for copy in copies:
        copy.wait_send()

    @pl.when(has_low)
    def _():
        down.wait_send()

    @pl.when(has_high)
    def _():
        up.wait_send()


def coarse_level(part, lat, edge, send, lists, ein, eout, nin, nout, bias, gain):
    groups = part.shape[0]
    rows, width = lat.shape
    rim = lists.shape[0] // 2
    return pl.pallas_call(
        coarse_kernel,
        in_specs=[pl.BlockSpec(memory_space=pltpu.VMEM)] * 11,
        out_specs=pl.BlockSpec(memory_space=pltpu.VMEM),
        out_shape=jax.ShapeDtypeStruct((rows, width), BF16),
        scratch_shapes=[
            pltpu.VMEM((groups - 1,) + part.shape[1:], BF16),
            pltpu.VMEM((edge.shape[0], 128), F32),
            pltpu.VMEM((edge.shape[0], 128), F32),
            pltpu.VMEM((2, rim, width), BF16),
            pltpu.VMEM((2, rim, width), BF16),
            pltpu.VMEM((DEG, rows, width), F32),
            pltpu.SemaphoreType.DMA((groups - 1,)),
            pltpu.SemaphoreType.DMA((groups - 1,)),
            pltpu.SemaphoreType.DMA((2,)),
            pltpu.SemaphoreType.DMA((2,)),
        ],
        compiler_params=pltpu.CompilerParams(
            vmem_limit_bytes=32 * 1024 * 1024, collective_id=0, has_side_effects=True
        ),
        cost_estimate=pl.CostEstimate(flops=1_500_000_000, bytes_accessed=3_000_000, transcendentals=0),
        name="coarse_level",
    )(part, lat, edge, send.reshape(rows, DEG), lists.reshape(2 * rim, 1),
      ein, eout, nin, nout, bias, gain)


def body(
    node_lat, edge_lat, edge_send, halo_list, pool_id,
    coarse_lat, cedge_lat, cedge_send, chalo_list,
    fine_edge_in, fine_edge_out, fine_node_in, fine_node_out, fine_bias, fine_gain,
    coarse_edge_in, coarse_edge_out, coarse_node_in, coarse_node_out, coarse_bias, coarse_gain,
):
    groups = lax.axis_size("group")
    clusters, width = coarse_lat.shape
    table, scale = front(halo_list, node_lat, fine_edge_in)
    table = table.reshape(table.shape[0], 1, table.shape[1])
    fine_out, part = fine_level(
        groups, clusters, edge_send, pool_id, table, scale, node_lat, edge_lat,
        fine_edge_in, fine_edge_out, fine_node_in, fine_node_out, fine_bias, fine_gain,
    )
    coarse_out = coarse_level(
        part, coarse_lat, cedge_lat, cedge_send, chalo_list,
        coarse_edge_in, coarse_edge_out, coarse_node_in, coarse_node_out, coarse_bias, coarse_gain,
    )
    return (fine_out, coarse_out)


def solution(mesh):
    both = ("group", "dom")
    rows, flat = P(both, None), P(both)
    placed = (rows, rows, flat, flat, flat, rows, rows, flat, flat) + (P(),) * 12
    return jax.shard_map(body, mesh=mesh, in_specs=placed, out_specs=(rows, rows), check_vma=False)
```

```python
import functools

import jax
import jax.numpy as jnp
from jax import lax
from jax.experimental import pallas as pl
from jax.experimental.pallas import tpu as pltpu
from jax.sharding import PartitionSpec as P

EPSILON = 1e-05
F32 = jnp.float32
BF16 = jnp.bfloat16
NT = 256
DEG = 4
VMEM = 60 * 1024 * 1024


def dot(a, b):
    return jnp.dot(a, b, preferred_element_type=F32)


def centre(weight):
    w = weight.astype(F32)
    return (w - jnp.mean(w, axis=-1, keepdims=True)).astype(BF16)


def unit_rows(z):
    return z * lax.rsqrt(jnp.mean(z * z, axis=-1, keepdims=True) + EPSILON)


def column(row):
    return jnp.broadcast_to(row, (128, 128)).T


def one_hot(names, starts):
    lane = lax.broadcasted_iota(jnp.int32, names.shape, 1)
    return jnp.concatenate(
        [jnp.where(names == lane + j, 1.0, 0.0).astype(BF16) for j in starts], axis=1
    )


def neighbours():
    here = lax.axis_index("dom")
    last = lax.axis_size("dom") - 1
    return here > 0, here < last, jnp.maximum(here - 1, 0), jnp.minimum(here + 1, last)


def rim_copies(rim_out, rim_in, rim_send, rim_recv, below, above):
    mine = lax.axis_index("group")
    return tuple(
        pltpu.make_async_remote_copy(
            src_ref=rim_out.at[i], dst_ref=rim_in.at[1 - i],
            send_sem=rim_send.at[i], recv_sem=rim_recv.at[i],
            device_id=(mine, to), device_id_type=pl.DeviceIdType.MESH,
        )
        for i, to in enumerate((below, above))
    )


def front_kernel(
    lists, pool, node, ein, table, scale, count, proj, rim_out, rim_in, rim_send, rim_recv
):
    rows, width = node.shape
    rim = rim_in.shape[1]
    mine = lax.axis_index("group")
    has_low, has_high, below, above = neighbours()
    barrier = pltpu.get_barrier_semaphore()

    @pl.when(has_low)
    def _():
        pl.semaphore_signal(
            barrier, inc=1, device_id=(mine, below), device_id_type=pl.DeviceIdType.MESH
        )

    @pl.when(has_high)
    def _():
        pl.semaphore_signal(
            barrier, inc=1, device_id=(mine, above), device_id_type=pl.DeviceIdType.MESH
        )

    @pl.when(jnp.logical_not(has_low))
    def _():
        rim_in[0] = jnp.zeros((rim, width), BF16)

    @pl.when(jnp.logical_not(has_high))
    def _():
        rim_in[1] = jnp.zeros((rim, width), BF16)

    down, up = rim_copies(rim_out, rim_in, rim_send, rim_recv, below, above)
    lane = lax.broadcasted_iota(jnp.int32, (128, 128), 1)

    def pick(side):
        for r in range(0, rim, 128):
            at = (side * rim + r) // 128
            chosen = one_hot(column(lists[at:at + 1, :]), range(0, rows, 128))
            rim_out[side, r:r + 128, :] = dot(chosen, node[...]).astype(BF16)

    pick(0)
    pl.semaphore_wait(barrier, has_low.astype(jnp.int32) + has_high.astype(jnp.int32))

    @pl.when(has_low)
    def _():
        down.start()

    pick(1)

    @pl.when(has_high)
    def _():
        up.start()

    top = jnp.full((1, width), 1e-20, F32)
    for r in range(0, rows, 256):
        p = dot(node[r:r + 256, :], ein[0])
        proj[rim + r:rim + r + 256, :] = p
        top = jnp.maximum(top, jnp.max(jnp.abs(p), axis=0, keepdims=True))

    for c in range(0, count.shape[1], 128):
        count[:, c:c + 128] = jnp.zeros((1, 128), F32)

    def tally(r, carry):
        names = column(pool[pl.ds(r, 1), :])
        for c in range(0, count.shape[1], 128):
            hit = jnp.where(names == lane + c, 1.0, 0.0)
            count[:, c:c + 128] += jnp.sum(hit, axis=0, keepdims=True)
        return carry

    lax.fori_loop(0, rows // 128, tally, 0)

    @pl.when(has_high)
    def _():
        down.wait_recv()

    @pl.when(has_low)
    def _():
        up.wait_recv()

    for side, start in ((0, 0), (1, rim + rows)):
        for r in range(0, rim, 256):
            p = dot(rim_in[side, r:r + 256, :], ein[0])
            proj[start + r:start + r + 256, :] = p
            top = jnp.maximum(top, jnp.max(jnp.abs(p), axis=0, keepdims=True))
    scale[...] = top * (1.0 / 32767.0)
    inv = 32767.0 / top
    for r in range(0, rows + 2 * rim, 256):
        q = jnp.round(proj[r:r + 256, :] * inv).astype(jnp.int32)
        table[r:r + 256, :] = (q[:, :128] & 0xFFFF) | (q[:, 128:] << 16)

    @pl.when(has_low)
    def _():
        down.wait_send()

    @pl.when(has_high)
    def _():
        up.wait_send()


def front(columns, lists, pool, node, ein):
    rows, width = node.shape
    rim = lists.shape[0] // 2
    return pl.pallas_call(
        front_kernel,
        in_specs=[pl.BlockSpec(memory_space=pltpu.VMEM)] * 4,
        out_specs=[pl.BlockSpec(memory_space=pltpu.VMEM)] * 3,
        out_shape=[jax.ShapeDtypeStruct((rows + 2 * rim, 128), jnp.int32),
                   jax.ShapeDtypeStruct((1, width), F32),
                   jax.ShapeDtypeStruct((1, columns), F32)],
        scratch_shapes=[
            pltpu.VMEM((rows + 2 * rim, width), F32),
            pltpu.VMEM((2, rim, width), BF16),
            pltpu.VMEM((2, rim, width), BF16),
            pltpu.SemaphoreType.DMA((2,)),
            pltpu.SemaphoreType.DMA((2,)),
        ],
        compiler_params=pltpu.CompilerParams(
            vmem_limit_bytes=VMEM, collective_id=1, has_side_effects=True
        ),
        cost_estimate=pl.CostEstimate(flops=1_500_000_000, bytes_accessed=3_000_000, transcendentals=0),
        name="front",
    )(lists.reshape(-1, 128), pool.reshape(-1, 128), node, ein)


def fine_kernel(
    groups, clusters,
    send, pool, count, table, scale, node, edge, ein, eout, nin, nout, bias, gain,
    out, part,
    gath, pre_lo, pre_hi, eoc, noc, bc, acc, held,
):
    step = pl.program_id(0)
    steps = pl.num_programs(0)
    et = NT * DEG
    first = step * et

    @pl.when(step == 0)
    def _():
        eoc[...] = centre(eout[...])
        noc[...] = centre(nout[...])
        b = bias[...]
        bc[...] = b - jnp.mean(b, axis=-1, keepdims=True)
        acc[...] = jnp.zeros_like(acc)
        held[...] = jnp.zeros_like(held)

    def gather(k):
        for n in range(NT):
            gath[pl.ds(k * NT + n, 1), :] = table[send[first + (n * DEG + k)]]

    def add_members(tile):
        ids = jnp.concatenate(
            [pool[pl.ds(tile * (NT // 128) + j, 1), :] for j in range(NT // 128)], axis=1
        )
        rows = held[...]
        for c in range(0, groups * clusters, 256):
            names = lax.broadcasted_iota(jnp.int32, (256, NT), 0) + c
            acc[c:c + 256, :] += dot(jnp.where(names == ids, 1.0, 0.0).astype(BF16), rows)

    gather(0)
    p = dot(edge[...], ein[2])
    pre_lo[...] = p[:, :128]
    pre_hi[...] = p[:, 128:]
    own = node[...]
    rv = dot(own, ein[1]) + bias[0:1, :]
    add_members(jnp.maximum(step - 1, 0))
    total = jnp.zeros((NT, 256), F32)
    for k in range(DEG):
        if k + 1 < DEG:
            gather(k + 1)
        g = gath[k * NT:(k + 1) * NT, :]
        s = jnp.concatenate([(g << 16) >> 16, g >> 16], axis=1).astype(F32) * scale[...]
        e = jnp.concatenate(
            [pre_lo[pl.ds(k, NT, stride=DEG), :], pre_hi[pl.ds(k, NT, stride=DEG), :]], axis=1
        )
        h = jnp.maximum(e + s + rv, 0.0).astype(BF16)
        total = total + unit_rows(dot(h, eoc[...]) + bc[1:2, :])
    summed = (total * gain[0:1, :]).astype(BF16)
    h = jnp.maximum(dot(own, nin[0]) + dot(summed, nin[1]) + bias[2:3, :], 0.0).astype(BF16)
    update = unit_rows(dot(h, noc[...]) + bc[3:4, :]) * gain[1:2, :]
    result = (own.astype(F32) + update).astype(BF16)
    out[...] = result
    held[...] = result

    @pl.when(step == steps - 1)
    def _():
        add_members(step)
        for g in range(groups):
            c = g * clusters
            part[g, 0:clusters, :] = acc[c:c + clusters, :].astype(BF16)
            n = count[:, c:c + clusters]
            big = jnp.floor(n * (1.0 / 256.0)) * 256.0
            which = lax.broadcasted_iota(jnp.int32, (16, clusters), 0)
            part[g, clusters:clusters + 16, :] = jnp.where(
                which == 0, n - big, jnp.where(which == 1, big, 0.0)
            ).astype(BF16)


def fine_level(groups, clusters, send, pool, count, table, scale, node, edge, ein, eout, nin, nout, bias, gain):
    rows, width = node.shape
    steps = rows // NT
    et = NT * DEG
    whole = pl.BlockSpec(memory_space=pltpu.VMEM)
    return pl.pallas_call(
        functools.partial(fine_kernel, groups, clusters),
        grid=(steps,),
        in_specs=[pl.BlockSpec(memory_space=pltpu.SMEM), whole, whole, whole, whole,
                  pl.BlockSpec((NT, width), lambda i: (i, 0)),
                  pl.BlockSpec((et, width), lambda i: (i, 0))] + [whole] * 6,
        out_specs=[pl.BlockSpec((NT, width), lambda i: (i, 0)),
                   pl.BlockSpec((groups, clusters + 16, width), lambda i: (0, 0, 0))],
        out_shape=[jax.ShapeDtypeStruct((rows, width), BF16),
                   jax.ShapeDtypeStruct((groups, clusters + 16, width), BF16)],
        scratch_shapes=[
            pltpu.VMEM((et, 128), jnp.int32),
            pltpu.VMEM((et, 128), F32),
            pltpu.VMEM((et, 128), F32),
            pltpu.VMEM((width, width), BF16),
            pltpu.VMEM((width, width), BF16),
            pltpu.VMEM((4, width), F32),
            pltpu.VMEM((groups * clusters, width), F32),
            pltpu.VMEM((NT, width), BF16),
        ],
        compiler_params=pltpu.CompilerParams(vmem_limit_bytes=VMEM),
        cost_estimate=pl.CostEstimate(flops=7_000_000_000, bytes_accessed=9_000_000, transcendentals=0),
        name="fine_level",
    )(send, pool.reshape(-1, 128), count, table, scale, node, edge, ein, eout, nin, nout, bias, gain)


def coarse_kernel(
    part, lat, edge, sends, lists, ein, eout, nin, nout, bias, gain,
    out,
    got, edges_lo, edges_hi, rim_out, rim_in, mix, names, sum_send, sum_recv, rim_send, rim_recv,
):
    groups = part.shape[0]
    rows, width = lat.shape
    rim = rim_in.shape[1]
    mine = lax.axis_index("group")
    here = lax.axis_index("dom")
    last = lax.axis_size("dom") - 1
    has_low = here > 0
    has_high = here < last
    below = jnp.maximum(here - 1, 0)
    above = jnp.minimum(here + 1, last)
    mesh_id = pl.DeviceIdType.MESH

    barrier = pltpu.get_barrier_semaphore()
    for o in range(1, groups):
        pl.semaphore_signal(
            barrier, inc=1, device_id=(lax.rem(mine + o, groups), here), device_id_type=mesh_id
        )

    @pl.when(has_low)
    def _():
        pl.semaphore_signal(barrier, inc=1, device_id=(mine, below), device_id_type=mesh_id)

    @pl.when(has_high)
    def _():
        pl.semaphore_signal(barrier, inc=1, device_id=(mine, above), device_id_type=mesh_id)

    pl.semaphore_wait(barrier, groups - 1 + has_low.astype(jnp.int32) + has_high.astype(jnp.int32))
    copies = []
    for o in range(1, groups):
        peer = lax.rem(mine + o, groups)
        copy = pltpu.make_async_remote_copy(
            src_ref=part.at[peer], dst_ref=got.at[o - 1],
            send_sem=sum_send.at[o - 1], recv_sem=sum_recv.at[o - 1],
            device_id=(peer, here), device_id_type=mesh_id,
        )
        copy.start()
        copies.append(copy)

    eoc = centre(eout[...])
    noc = centre(nout[...])
    b = bias[...]
    bc = b - jnp.mean(b, axis=-1, keepdims=True)
    for r in range(0, edge.shape[0], 256):
        p = dot(edge[r:r + 256, :], ein[2])
        edges_lo[r:r + 256, :] = p[:, :128]
        edges_hi[r:r + 256, :] = p[:, 128:]
    for r in range(sends.shape[0]):
        names[r * 128:(r + 1) * 128, :] = column(sends[r:r + 1, :])
    sums = part[mine].astype(F32)
    for copy in copies:
        copy.wait_recv()
    for o in range(1, groups):
        sums = sums + got[o - 1].astype(F32)
    members = sums[rows:rows + 1, :] + sums[rows + 1:rows + 2, :]
    inv = jnp.broadcast_to(1.0 / jnp.maximum(members, 1.0), (128, rows)).T
    inv = jnp.concatenate([inv] * (width // 128), axis=1)
    own = (lat[...].astype(F32) + sums[:rows, :] * inv).astype(BF16)
    picks = jnp.concatenate([column(lists[r:r + 1, :]) for r in range(lists.shape[0])], axis=0)
    chosen = one_hot(picks, range(0, rows, 128))
    border_rows = dot(chosen, own).astype(BF16)
    rim_out[0] = border_rows[:rim, :]
    rim_out[1] = border_rows[rim:, :]
    down = pltpu.make_async_remote_copy(
        src_ref=rim_out.at[0], dst_ref=rim_in.at[1],
        send_sem=rim_send.at[0], recv_sem=rim_recv.at[0],
        device_id=(mine, below), device_id_type=mesh_id,
    )
    up = pltpu.make_async_remote_copy(
        src_ref=rim_out.at[1], dst_ref=rim_in.at[0],
        send_sem=rim_send.at[1], recv_sem=rim_recv.at[1],
        device_id=(mine, above), device_id_type=mesh_id,
    )

    @pl.when(has_low)
    def _():
        down.start()

    @pl.when(has_high)
    def _():
        up.start()

    @pl.when(jnp.logical_not(has_low))
    def _():
        rim_in[0] = jnp.zeros((rim, width), BF16)

    @pl.when(jnp.logical_not(has_high))
    def _():
        rim_in[1] = jnp.zeros((rim, width), BF16)

    sender = dot(own, ein[0]).astype(BF16)
    recv = dot(own, ein[1]) + b[0:1, :]
    npre = dot(own, nin[0]) + b[2:3, :]
    inner = range(rim, rim + rows, 128)
    outer = list(range(0, rim, 128)) + list(range(rim + rows, 2 * rim + rows, 128))
    for k in range(DEG):
        member = one_hot(names[pl.ds(k, rows, stride=DEG), :], inner)
        e = jnp.concatenate(
            [edges_lo[pl.ds(k, rows, stride=DEG), :], edges_hi[pl.ds(k, rows, stride=DEG), :]],
            axis=1,
        )
        mix[k] = e + recv + dot(member, sender)

    @pl.when(has_high)
    def _():
        down.wait_recv()

    @pl.when(has_low)
    def _():
        up.wait_recv()

    low = dot(rim_in[0], ein[0]).astype(BF16)
    high = dot(rim_in[1], ein[0]).astype(BF16)
    rims = jnp.concatenate([low, high], axis=0)
    total = jnp.zeros((rows, width), F32)
    for k in range(DEG):
        member = one_hot(names[pl.ds(k, rows, stride=DEG), :], outer)
        h = jnp.maximum(mix[k] + dot(member, rims), 0.0).astype(BF16)
        total = total + unit_rows(dot(h, eoc) + bc[1:2, :])
    summed = (total * gain[0:1, :]).astype(BF16)
    h = jnp.maximum(npre + dot(summed, nin[1]), 0.0).astype(BF16)
    update = unit_rows(dot(h, noc) + bc[3:4, :]) * gain[1:2, :]
    out[...] = (own.astype(F32) + update).astype(BF16)
    for copy in copies:
        copy.wait_send()

    @pl.when(has_low)
    def _():
        down.wait_send()

    @pl.when(has_high)
    def _():
        up.wait_send()


def coarse_level(part, lat, edge, send, lists, ein, eout, nin, nout, bias, gain):
    groups = part.shape[0]
    rows, width = lat.shape
    rim = lists.shape[0] // 2
    return pl.pallas_call(
        coarse_kernel,
        in_specs=[pl.BlockSpec(memory_space=pltpu.VMEM)] * 11,
        out_specs=pl.BlockSpec(memory_space=pltpu.VMEM),
        out_shape=jax.ShapeDtypeStruct((rows, width), BF16),
        scratch_shapes=[
            pltpu.VMEM((groups - 1,) + part.shape[1:], BF16),
            pltpu.VMEM((edge.shape[0], 128), F32),
            pltpu.VMEM((edge.shape[0], 128), F32),
            pltpu.VMEM((2, rim, width), BF16),
            pltpu.VMEM((2, rim, width), BF16),
            pltpu.VMEM((DEG, rows, width), F32),
            pltpu.VMEM((edge.shape[0], 128), jnp.int32),
            pltpu.SemaphoreType.DMA((groups - 1,)),
            pltpu.SemaphoreType.DMA((groups - 1,)),
            pltpu.SemaphoreType.DMA((2,)),
            pltpu.SemaphoreType.DMA((2,)),
        ],
        compiler_params=pltpu.CompilerParams(
            vmem_limit_bytes=VMEM, collective_id=0, has_side_effects=True
        ),
        cost_estimate=pl.CostEstimate(flops=1_500_000_000, bytes_accessed=3_000_000, transcendentals=0),
        name="coarse_level",
    )(part, lat, edge, send.reshape(-1, 128), lists.reshape(-1, 128),
      ein, eout, nin, nout, bias, gain)


def body(
    node_lat, edge_lat, edge_send, halo_list, pool_id,
    coarse_lat, cedge_lat, cedge_send, chalo_list,
    fine_edge_in, fine_edge_out, fine_node_in, fine_node_out, fine_bias, fine_gain,
    coarse_edge_in, coarse_edge_out, coarse_node_in, coarse_node_out, coarse_bias, coarse_gain,
):
    groups = lax.axis_size("group")
    clusters, width = coarse_lat.shape
    table, scale, count = front(groups * clusters, halo_list, pool_id, node_lat, fine_edge_in)
    table = table.reshape(table.shape[0], 1, table.shape[1])
    fine_out, part = fine_level(
        groups, clusters, edge_send, pool_id, count, table, scale, node_lat, edge_lat,
        fine_edge_in, fine_edge_out, fine_node_in, fine_node_out, fine_bias, fine_gain,
    )
    coarse_out = coarse_level(
        part, coarse_lat, cedge_lat, cedge_send, chalo_list,
        coarse_edge_in, coarse_edge_out, coarse_node_in, coarse_node_out, coarse_bias, coarse_gain,
    )
    return (fine_out, coarse_out)


def solution(mesh):
    both = ("group", "dom")
    rows, flat = P(both, None), P(both)
    placed = (rows, rows, flat, flat, flat, rows, rows, flat, flat) + (P(),) * 12
    return jax.shard_map(body, mesh=mesh, in_specs=placed, out_specs=(rows, rows), check_vma=False)
```

```python
import functools

import jax
import jax.numpy as jnp
from jax import lax
from jax.experimental import pallas as pl
from jax.experimental.pallas import tpu as pltpu
from jax.sharding import PartitionSpec as P

EPSILON = 1e-05
F32 = jnp.float32
BF16 = jnp.bfloat16
NT = 256
DEG = 4
BATCH = 16
PIECES = 2
VMEM = 60 * 1024 * 1024


def dot(a, b):
    return jnp.dot(a, b, preferred_element_type=F32)


def centre(weight):
    w = weight.astype(F32)
    return (w - jnp.mean(w, axis=-1, keepdims=True)).astype(BF16)


def unit_rows(z):
    return z * lax.rsqrt(jnp.mean(z * z, axis=-1, keepdims=True) + EPSILON)


def column(row):
    return jnp.broadcast_to(row, (128, 128)).T


def one_hot(names, starts):
    lane = lax.broadcasted_iota(jnp.int32, names.shape, 1)
    return jnp.concatenate(
        [jnp.where(names == lane + j, 1.0, 0.0).astype(BF16) for j in starts], axis=1
    )


def neighbours():
    here = lax.axis_index("dom")
    last = lax.axis_size("dom") - 1
    return here > 0, here < last, jnp.maximum(here - 1, 0), jnp.minimum(here + 1, last)


def rim_copies(rim_out, rim_in, rim_send, rim_recv, below, above):
    mine = lax.axis_index("group")
    size = rim_out.shape[1] // PIECES
    return [
        [
            pltpu.make_async_remote_copy(
                src_ref=rim_out.at[i, pl.ds(p * size, size)],
                dst_ref=rim_in.at[1 - i, pl.ds(p * size, size)],
                send_sem=rim_send.at[i, p], recv_sem=rim_recv.at[i, p],
                device_id=(mine, to), device_id_type=pl.DeviceIdType.MESH,
            )
            for p in range(PIECES)
        ]
        for i, to in enumerate((below, above))
    ]


def front_kernel(
    lists, pool, node, ein, table, scale, count, proj, rim_out, rim_in, rim_send, rim_recv
):
    rows, width = node.shape
    rim = rim_in.shape[1]
    mine = lax.axis_index("group")
    has_low, has_high, below, above = neighbours()
    barrier = pltpu.get_barrier_semaphore()

    @pl.when(has_low)
    def _():
        pl.semaphore_signal(
            barrier, inc=1, device_id=(mine, below), device_id_type=pl.DeviceIdType.MESH
        )

    @pl.when(has_high)
    def _():
        pl.semaphore_signal(
            barrier, inc=1, device_id=(mine, above), device_id_type=pl.DeviceIdType.MESH
        )

    @pl.when(jnp.logical_not(has_low))
    def _():
        rim_in[0] = jnp.zeros((rim, width), BF16)

    @pl.when(jnp.logical_not(has_high))
    def _():
        rim_in[1] = jnp.zeros((rim, width), BF16)

    down, up = rim_copies(rim_out, rim_in, rim_send, rim_recv, below, above)
    lane = lax.broadcasted_iota(jnp.int32, (128, 128), 1)

    size = rim // PIECES

    def pick(side, piece):
        for r in range(piece * size, (piece + 1) * size, 128):
            at = (side * rim + r) // 128
            chosen = one_hot(column(lists[at:at + 1, :]), range(0, rows, 128))
            rim_out[side, r:r + 128, :] = dot(chosen, node[...]).astype(BF16)

    pick(0, 0)
    pl.semaphore_wait(barrier, has_low.astype(jnp.int32) + has_high.astype(jnp.int32))
    for piece in range(PIECES):
        if piece:
            pick(0, piece)

        @pl.when(has_low)
        def _():
            down[piece].start()

        pick(1, piece)

        @pl.when(has_high)
        def _():
            up[piece].start()

    top = jnp.full((1, width), 1e-20, F32)
    for r in range(0, rows, 256):
        p = dot(node[r:r + 256, :], ein[0])
        proj[rim + r:rim + r + 256, :] = p
        top = jnp.maximum(top, jnp.max(jnp.abs(p), axis=0, keepdims=True))

    for c in range(0, count.shape[1], 128):
        count[:, c:c + 128] = jnp.zeros((1, 128), F32)

    def tally(r, carry):
        names = column(pool[pl.ds(r, 1), :])
        for c in range(0, count.shape[1], 128):
            hit = jnp.where(names == lane + c, 1.0, 0.0)
            count[:, c:c + 128] += jnp.sum(hit, axis=0, keepdims=True)
        return carry

    lax.fori_loop(0, rows // 128, tally, 0)

    for piece in range(PIECES):
        for side, start, there, copies in ((1, rim + rows, has_high, down), (0, 0, has_low, up)):

            @pl.when(there)
            def _():
                copies[piece].wait_recv()

            for r in range(piece * size, (piece + 1) * size, 256):
                p = dot(rim_in[side, r:r + 256, :], ein[0])
                proj[start + r:start + r + 256, :] = p
                top = jnp.maximum(top, jnp.max(jnp.abs(p), axis=0, keepdims=True))
    scale[...] = top * (1.0 / 32767.0)
    inv = 32767.0 / top
    for r in range(0, rows + 2 * rim, 256):
        q = jnp.round(proj[r:r + 256, :] * inv).astype(jnp.int32)
        table[r:r + 256, :] = (q[:, :128] & 0xFFFF) | (q[:, 128:] << 16)

    for piece in range(PIECES):

        @pl.when(has_low)
        def _():
            down[piece].wait_send()

        @pl.when(has_high)
        def _():
            up[piece].wait_send()


def front(columns, lists, pool, node, ein):
    rows, width = node.shape
    rim = lists.shape[0] // 2
    return pl.pallas_call(
        front_kernel,
        in_specs=[pl.BlockSpec(memory_space=pltpu.VMEM)] * 4,
        out_specs=[pl.BlockSpec(memory_space=pltpu.VMEM)] * 3,
        out_shape=[jax.ShapeDtypeStruct((rows + 2 * rim, 128), jnp.int32),
                   jax.ShapeDtypeStruct((1, width), F32),
                   jax.ShapeDtypeStruct((1, columns), F32)],
        scratch_shapes=[
            pltpu.VMEM((rows + 2 * rim, width), F32),
            pltpu.VMEM((2, rim, width), BF16),
            pltpu.VMEM((2, rim, width), BF16),
            pltpu.SemaphoreType.DMA((2, PIECES)),
            pltpu.SemaphoreType.DMA((2, PIECES)),
        ],
        compiler_params=pltpu.CompilerParams(
            vmem_limit_bytes=VMEM, collective_id=1, has_side_effects=True
        ),
        cost_estimate=pl.CostEstimate(flops=1_500_000_000, bytes_accessed=3_000_000, transcendentals=0),
        name="front",
    )(lists.reshape(-1, 128), pool.reshape(-1, 128), node, ein)


def fine_kernel(
    groups, clusters,
    send, pool, count, table, scale, node, edge, ein, eout, nin, nout, bias, gain,
    out, part,
    gath, pre_lo, pre_hi, eoc, noc, bc, acc, held,
):
    step = pl.program_id(0)
    steps = pl.num_programs(0)
    et = NT * DEG
    first = step * et

    @pl.when(step == 0)
    def _():
        eoc[...] = centre(eout[...])
        noc[...] = centre(nout[...])
        b = bias[...]
        bc[...] = b - jnp.mean(b, axis=-1, keepdims=True)
        acc[...] = jnp.zeros_like(acc)
        held[...] = jnp.zeros_like(held)

    def gather(k):
        for n in range(0, NT, BATCH):
            got = [table[send[first + ((n + j) * DEG + k)]] for j in range(BATCH)]
            for j in range(BATCH):
                gath[pl.ds(k * NT + n + j, 1), :] = got[j]

    def add_members(tile):
        ids = jnp.concatenate(
            [pool[pl.ds(tile * (NT // 128) + j, 1), :] for j in range(NT // 128)], axis=1
        )
        rows = held[...]
        for c in range(0, groups * clusters, 256):
            names = lax.broadcasted_iota(jnp.int32, (256, NT), 0) + c
            acc[c:c + 256, :] += dot(jnp.where(names == ids, 1.0, 0.0).astype(BF16), rows)

    gather(0)
    p = dot(edge[...], ein[2])
    pre_lo[...] = p[:, :128]
    pre_hi[...] = p[:, 128:]
    own = node[...]
    rv = dot(own, ein[1]) + bias[0:1, :]
    add_members(jnp.maximum(step - 1, 0))
    total = jnp.zeros((NT, 256), F32)
    for k in range(DEG):
        if k + 1 < DEG:
            gather(k + 1)
        g = gath[k * NT:(k + 1) * NT, :]
        s = jnp.concatenate([(g << 16) >> 16, g >> 16], axis=1).astype(F32) * scale[...]
        e = jnp.concatenate(
            [pre_lo[pl.ds(k, NT, stride=DEG), :], pre_hi[pl.ds(k, NT, stride=DEG), :]], axis=1
        )
        h = jnp.maximum(e + s + rv, 0.0).astype(BF16)
        total = total + unit_rows(dot(h, eoc[...]) + bc[1:2, :])
    summed = (total * gain[0:1, :]).astype(BF16)
    h = jnp.maximum(dot(own, nin[0]) + dot(summed, nin[1]) + bias[2:3, :], 0.0).astype(BF16)
    update = unit_rows(dot(h, noc[...]) + bc[3:4, :]) * gain[1:2, :]
    result = (own.astype(F32) + update).astype(BF16)
    out[...] = result
    held[...] = result

    @pl.when(step == steps - 1)
    def _():
        add_members(step)
        for g in range(groups):
            c = g * clusters
            part[g, 0:clusters, :] = acc[c:c + clusters, :].astype(BF16)
            n = count[:, c:c + clusters]
            big = jnp.floor(n * (1.0 / 256.0)) * 256.0
            which = lax.broadcasted_iota(jnp.int32, (16, clusters), 0)
            part[g, clusters:clusters + 16, :] = jnp.where(
                which == 0, n - big, jnp.where(which == 1, big, 0.0)
            ).astype(BF16)


def fine_level(groups, clusters, send, pool, count, table, scale, node, edge, ein, eout, nin, nout, bias, gain):
    rows, width = node.shape
    steps = rows // NT
    et = NT * DEG
    whole = pl.BlockSpec(memory_space=pltpu.VMEM)
    return pl.pallas_call(
        functools.partial(fine_kernel, groups, clusters),
        grid=(steps,),
        in_specs=[pl.BlockSpec(memory_space=pltpu.SMEM), whole, whole, whole, whole,
                  pl.BlockSpec((NT, width), lambda i: (i, 0)),
                  pl.BlockSpec((et, width), lambda i: (i, 0))] + [whole] * 6,
        out_specs=[pl.BlockSpec((NT, width), lambda i: (i, 0)),
                   pl.BlockSpec((groups, clusters + 16, width), lambda i: (0, 0, 0))],
        out_shape=[jax.ShapeDtypeStruct((rows, width), BF16),
                   jax.ShapeDtypeStruct((groups, clusters + 16, width), BF16)],
        scratch_shapes=[
            pltpu.VMEM((et, 128), jnp.int32),
            pltpu.VMEM((et, 128), F32),
            pltpu.VMEM((et, 128), F32),
            pltpu.VMEM((width, width), BF16),
            pltpu.VMEM((width, width), BF16),
            pltpu.VMEM((4, width), F32),
            pltpu.VMEM((groups * clusters, width), F32),
            pltpu.VMEM((NT, width), BF16),
        ],
        compiler_params=pltpu.CompilerParams(vmem_limit_bytes=VMEM),
        cost_estimate=pl.CostEstimate(flops=7_000_000_000, bytes_accessed=9_000_000, transcendentals=0),
        name="fine_level",
    )(send, pool.reshape(-1, 128), count, table, scale, node, edge, ein, eout, nin, nout, bias, gain)


def coarse_kernel(
    part, lat, edge, sends, lists, ein, eout, nin, nout, bias, gain,
    out,
    got, edges_lo, edges_hi, rim_out, rim_in, mix, names, near, far, chosen, sum_send, sum_recv, rim_send, rim_recv,
):
    groups = part.shape[0]
    rows, width = lat.shape
    rim = rim_in.shape[1]
    mine = lax.axis_index("group")
    here = lax.axis_index("dom")
    last = lax.axis_size("dom") - 1
    has_low = here > 0
    has_high = here < last
    below = jnp.maximum(here - 1, 0)
    above = jnp.minimum(here + 1, last)
    mesh_id = pl.DeviceIdType.MESH

    barrier = pltpu.get_barrier_semaphore()
    for o in range(1, groups):
        pl.semaphore_signal(
            barrier, inc=1, device_id=(lax.rem(mine + o, groups), here), device_id_type=mesh_id
        )

    @pl.when(has_low)
    def _():
        pl.semaphore_signal(barrier, inc=1, device_id=(mine, below), device_id_type=mesh_id)

    @pl.when(has_high)
    def _():
        pl.semaphore_signal(barrier, inc=1, device_id=(mine, above), device_id_type=mesh_id)

    pl.semaphore_wait(barrier, groups - 1 + has_low.astype(jnp.int32) + has_high.astype(jnp.int32))
    copies = []
    for o in range(1, groups):
        peer = lax.rem(mine + o, groups)
        copy = pltpu.make_async_remote_copy(
            src_ref=part.at[peer], dst_ref=got.at[o - 1],
            send_sem=sum_send.at[o - 1], recv_sem=sum_recv.at[o - 1],
            device_id=(peer, here), device_id_type=mesh_id,
        )
        copy.start()
        copies.append(copy)

    eoc = centre(eout[...])
    noc = centre(nout[...])
    b = bias[...]
    bc = b - jnp.mean(b, axis=-1, keepdims=True)
    for r in range(0, edge.shape[0], 256):
        p = dot(edge[r:r + 256, :], ein[2])
        edges_lo[r:r + 256, :] = p[:, :128]
        edges_hi[r:r + 256, :] = p[:, 128:]
    for r in range(sends.shape[0]):
        names[r * 128:(r + 1) * 128, :] = column(sends[r:r + 1, :])
    for k in range(DEG):
        at = names[pl.ds(k, rows, stride=DEG), :]
        near[k] = one_hot(at, range(rim, rim + rows, 128))
        far[k] = one_hot(
            at, list(range(0, rim, 128)) + list(range(rim + rows, 2 * rim + rows, 128))
        )
    picks = jnp.concatenate([column(lists[r:r + 1, :]) for r in range(lists.shape[0])], axis=0)
    chosen[...] = one_hot(picks, range(0, rows, 128))
    sums = part[mine].astype(F32)
    for copy in copies:
        copy.wait_recv()
    for o in range(1, groups):
        sums = sums + got[o - 1].astype(F32)
    members = sums[rows:rows + 1, :] + sums[rows + 1:rows + 2, :]
    inv = jnp.broadcast_to(1.0 / jnp.maximum(members, 1.0), (128, rows)).T
    inv = jnp.concatenate([inv] * (width // 128), axis=1)
    own = (lat[...].astype(F32) + sums[:rows, :] * inv).astype(BF16)
    border_rows = dot(chosen[...], own).astype(BF16)
    rim_out[0] = border_rows[:rim, :]
    rim_out[1] = border_rows[rim:, :]
    down = pltpu.make_async_remote_copy(
        src_ref=rim_out.at[0], dst_ref=rim_in.at[1],
        send_sem=rim_send.at[0], recv_sem=rim_recv.at[0],
        device_id=(mine, below), device_id_type=mesh_id,
    )
    up = pltpu.make_async_remote_copy(
        src_ref=rim_out.at[1], dst_ref=rim_in.at[0],
        send_sem=rim_send.at[1], recv_sem=rim_recv.at[1],
        device_id=(mine, above), device_id_type=mesh_id,
    )

    @pl.when(has_low)
    def _():
        down.start()

    @pl.when(has_high)
    def _():
        up.start()

    @pl.when(jnp.logical_not(has_low))
    def _():
        rim_in[0] = jnp.zeros((rim, width), BF16)

    @pl.when(jnp.logical_not(has_high))
    def _():
        rim_in[1] = jnp.zeros((rim, width), BF16)

    sender = dot(own, ein[0]).astype(BF16)
    recv = dot(own, ein[1]) + b[0:1, :]
    npre = dot(own, nin[0]) + b[2:3, :]
    for k in range(DEG):
        e = jnp.concatenate(
            [edges_lo[pl.ds(k, rows, stride=DEG), :], edges_hi[pl.ds(k, rows, stride=DEG), :]],
            axis=1,
        )
        mix[k] = e + recv + dot(near[k], sender)

    @pl.when(has_high)
    def _():
        down.wait_recv()

    @pl.when(has_low)
    def _():
        up.wait_recv()

    low = dot(rim_in[0], ein[0]).astype(BF16)
    high = dot(rim_in[1], ein[0]).astype(BF16)
    rims = jnp.concatenate([low, high], axis=0)
    total = jnp.zeros((rows, width), F32)
    for k in range(DEG):
        h = jnp.maximum(mix[k] + dot(far[k], rims), 0.0).astype(BF16)
        total = total + unit_rows(dot(h, eoc) + bc[1:2, :])
    summed = (total * gain[0:1, :]).astype(BF16)
    h = jnp.maximum(npre + dot(summed, nin[1]), 0.0).astype(BF16)
    update = unit_rows(dot(h, noc) + bc[3:4, :]) * gain[1:2, :]
    out[...] = own.astype(F32) + update
    for copy in copies:
        copy.wait_send()

    @pl.when(has_low)
    def _():
        down.wait_send()

    @pl.when(has_high)
    def _():
        up.wait_send()


def coarse_level(part, lat, edge, send, lists, ein, eout, nin, nout, bias, gain):
    groups = part.shape[0]
    rows, width = lat.shape
    rim = lists.shape[0] // 2
    return pl.pallas_call(
        coarse_kernel,
        in_specs=[pl.BlockSpec(memory_space=pltpu.VMEM)] * 11,
        out_specs=pl.BlockSpec(memory_space=pltpu.VMEM),
        out_shape=jax.ShapeDtypeStruct((rows, width), F32),
        scratch_shapes=[
            pltpu.VMEM((groups - 1,) + part.shape[1:], BF16),
            pltpu.VMEM((edge.shape[0], 128), F32),
            pltpu.VMEM((edge.shape[0], 128), F32),
            pltpu.VMEM((2, rim, width), BF16),
            pltpu.VMEM((2, rim, width), BF16),
            pltpu.VMEM((DEG, rows, width), F32),
            pltpu.VMEM((edge.shape[0], 128), jnp.int32),
            pltpu.VMEM((DEG, rows, rows), BF16),
            pltpu.VMEM((DEG, rows, 2 * rim), BF16),
            pltpu.VMEM((2 * rim, rows), BF16),
            pltpu.SemaphoreType.DMA((groups - 1,)),
            pltpu.SemaphoreType.DMA((groups - 1,)),
            pltpu.SemaphoreType.DMA((2,)),
            pltpu.SemaphoreType.DMA((2,)),
        ],
        compiler_params=pltpu.CompilerParams(
            vmem_limit_bytes=VMEM, collective_id=0, has_side_effects=True
        ),
        cost_estimate=pl.CostEstimate(flops=1_500_000_000, bytes_accessed=3_000_000, transcendentals=0),
        name="coarse_level",
    )(part, lat, edge, send.reshape(-1, 128), lists.reshape(-1, 128),
      ein, eout, nin, nout, bias, gain)


def body(
    node_lat, edge_lat, edge_send, halo_list, pool_id,
    coarse_lat, cedge_lat, cedge_send, chalo_list,
    fine_edge_in, fine_edge_out, fine_node_in, fine_node_out, fine_bias, fine_gain,
    coarse_edge_in, coarse_edge_out, coarse_node_in, coarse_node_out, coarse_bias, coarse_gain,
):
    groups = lax.axis_size("group")
    clusters, width = coarse_lat.shape
    table, scale, count = front(groups * clusters, halo_list, pool_id, node_lat, fine_edge_in)
    table = table.reshape(table.shape[0], 1, table.shape[1])
    fine_out, part = fine_level(
        groups, clusters, edge_send, pool_id, count, table, scale, node_lat, edge_lat,
        fine_edge_in, fine_edge_out, fine_node_in, fine_node_out, fine_bias, fine_gain,
    )
    coarse_out = coarse_level(
        part, coarse_lat, cedge_lat, cedge_send, chalo_list,
        coarse_edge_in, coarse_edge_out, coarse_node_in, coarse_node_out, coarse_bias, coarse_gain,
    )
    return (fine_out, coarse_out.astype(BF16))


def solution(mesh):
    both = ("group", "dom")
    rows, flat = P(both, None), P(both)
    placed = (rows, rows, flat, flat, flat, rows, rows, flat, flat) + (P(),) * 12
    return jax.shard_map(body, mesh=mesh, in_specs=placed, out_specs=(rows, rows), check_vma=False)
```

```python
import functools

import jax
import jax.numpy as jnp
from jax import lax
from jax.experimental import pallas as pl
from jax.experimental.pallas import tpu as pltpu
from jax.sharding import PartitionSpec as P

EPSILON = 1e-05
F32 = jnp.float32
BF16 = jnp.bfloat16
NT = 256
DEG = 4
BATCH = 16
PIECES = 2
VMEM = 60 * 1024 * 1024


def dot(a, b):
    return jnp.dot(a, b, preferred_element_type=F32)


def centre(weight):
    w = weight.astype(F32)
    return (w - jnp.mean(w, axis=-1, keepdims=True)).astype(BF16)


def unit_rows(z):
    width = z.shape[1]
    ones = jnp.full((width, 128), 1.0, BF16)
    square = dot((z * z).astype(BF16), ones) * (1.0 / width)
    return z * jnp.concatenate([lax.rsqrt(square + EPSILON)] * (width // 128), axis=1)


def column(row):
    return jnp.broadcast_to(row, (128, 128)).T


def one_hot(names, starts):
    lane = lax.broadcasted_iota(jnp.int32, names.shape, 1)
    return jnp.concatenate(
        [jnp.where(names == lane + j, 1.0, 0.0).astype(BF16) for j in starts], axis=1
    )


def neighbours():
    here = lax.axis_index("dom")
    last = lax.axis_size("dom") - 1
    return here > 0, here < last, jnp.maximum(here - 1, 0), jnp.minimum(here + 1, last)


def rim_copies(rim_out, rim_in, rim_send, rim_recv, below, above):
    mine = lax.axis_index("group")
    size = rim_out.shape[1] // PIECES
    return [
        [
            pltpu.make_async_remote_copy(
                src_ref=rim_out.at[i, pl.ds(p * size, size)],
                dst_ref=rim_in.at[1 - i, pl.ds(p * size, size)],
                send_sem=rim_send.at[i, p], recv_sem=rim_recv.at[i, p],
                device_id=(mine, to), device_id_type=pl.DeviceIdType.MESH,
            )
            for p in range(PIECES)
        ]
        for i, to in enumerate((below, above))
    ]


def front_kernel(
    lists, pool, node, ein, table, scale, count, proj, rim_out, rim_in, rim_send, rim_recv
):
    rows, width = node.shape
    rim = rim_in.shape[1]
    mine = lax.axis_index("group")
    has_low, has_high, below, above = neighbours()
    barrier = pltpu.get_barrier_semaphore()

    @pl.when(has_low)
    def _():
        pl.semaphore_signal(
            barrier, inc=1, device_id=(mine, below), device_id_type=pl.DeviceIdType.MESH
        )

    @pl.when(has_high)
    def _():
        pl.semaphore_signal(
            barrier, inc=1, device_id=(mine, above), device_id_type=pl.DeviceIdType.MESH
        )

    @pl.when(jnp.logical_not(has_low))
    def _():
        rim_in[0] = jnp.zeros((rim, width), BF16)

    @pl.when(jnp.logical_not(has_high))
    def _():
        rim_in[1] = jnp.zeros((rim, width), BF16)

    down, up = rim_copies(rim_out, rim_in, rim_send, rim_recv, below, above)
    lane = lax.broadcasted_iota(jnp.int32, (128, 128), 1)

    size = rim // PIECES

    def pick(side, piece):
        for r in range(piece * size, (piece + 1) * size, 128):
            at = (side * rim + r) // 128
            chosen = one_hot(column(lists[at:at + 1, :]), range(0, rows, 128))
            rim_out[side, r:r + 128, :] = dot(chosen, node[...]).astype(BF16)

    pick(0, 0)
    pl.semaphore_wait(barrier, has_low.astype(jnp.int32) + has_high.astype(jnp.int32))
    for piece in range(PIECES):
        if piece:
            pick(0, piece)

        @pl.when(has_low)
        def _():
            down[piece].start()

        pick(1, piece)

        @pl.when(has_high)
        def _():
            up[piece].start()

    top = jnp.full((1, width), 1e-20, F32)
    for r in range(0, rows, 256):
        p = dot(node[r:r + 256, :], ein[0])
        proj[rim + r:rim + r + 256, :] = p
        top = jnp.maximum(top, jnp.max(jnp.abs(p), axis=0, keepdims=True))

    for c in range(0, count.shape[1], 128):
        count[:, c:c + 128] = jnp.zeros((1, 128), F32)

    def tally(r, carry):
        names = column(pool[pl.ds(r, 1), :])
        for c in range(0, count.shape[1], 128):
            hit = jnp.where(names == lane + c, 1.0, 0.0)
            count[:, c:c + 128] += jnp.sum(hit, axis=0, keepdims=True)
        return carry

    lax.fori_loop(0, rows // 128, tally, 0)

    for piece in range(PIECES):
        for side, start, there, copies in ((1, rim + rows, has_high, down), (0, 0, has_low, up)):

            @pl.when(there)
            def _():
                copies[piece].wait_recv()

            for r in range(piece * size, (piece + 1) * size, 256):
                p = dot(rim_in[side, r:r + 256, :], ein[0])
                proj[start + r:start + r + 256, :] = p
                top = jnp.maximum(top, jnp.max(jnp.abs(p), axis=0, keepdims=True))
    scale[...] = top * (1.0 / 32767.0)
    inv = 32767.0 / top
    for r in range(0, rows + 2 * rim, 256):
        q = jnp.round(proj[r:r + 256, :] * inv).astype(jnp.int32)
        table[r:r + 256, :] = (q[:, :128] & 0xFFFF) | (q[:, 128:] << 16)

    for piece in range(PIECES):

        @pl.when(has_low)
        def _():
            down[piece].wait_send()

        @pl.when(has_high)
        def _():
            up[piece].wait_send()


def front(columns, lists, pool, node, ein):
    rows, width = node.shape
    rim = lists.shape[0] // 2
    return pl.pallas_call(
        front_kernel,
        in_specs=[pl.BlockSpec(memory_space=pltpu.VMEM)] * 4,
        out_specs=[pl.BlockSpec(memory_space=pltpu.VMEM)] * 3,
        out_shape=[jax.ShapeDtypeStruct((rows + 2 * rim, 128), jnp.int32),
                   jax.ShapeDtypeStruct((1, width), F32),
                   jax.ShapeDtypeStruct((1, columns), F32)],
        scratch_shapes=[
            pltpu.VMEM((rows + 2 * rim, width), F32),
            pltpu.VMEM((2, rim, width), BF16),
            pltpu.VMEM((2, rim, width), BF16),
            pltpu.SemaphoreType.DMA((2, PIECES)),
            pltpu.SemaphoreType.DMA((2, PIECES)),
        ],
        compiler_params=pltpu.CompilerParams(
            vmem_limit_bytes=VMEM, collective_id=1, has_side_effects=True
        ),
        cost_estimate=pl.CostEstimate(flops=1_500_000_000, bytes_accessed=3_000_000, transcendentals=0),
        name="front",
    )(lists.reshape(-1, 128), pool.reshape(-1, 128), node, ein)


def fine_kernel(
    groups, clusters,
    send, pool, count, table, scale, node, edge, ein, eout, nin, nout, bias, gain,
    out, part,
    gath, pre_lo, pre_hi, eoc, noc, bc, acc, held,
):
    step = pl.program_id(0)
    steps = pl.num_programs(0)
    et = NT * DEG
    first = step * et

    @pl.when(step == 0)
    def _():
        eoc[...] = centre(eout[...])
        noc[...] = centre(nout[...])
        b = bias[...]
        bc[...] = b - jnp.mean(b, axis=-1, keepdims=True)
        acc[...] = jnp.zeros_like(acc)
        held[...] = jnp.zeros_like(held)

    def gather(k):
        for n in range(0, NT, BATCH):
            got = [table[send[first + ((n + j) * DEG + k)]] for j in range(BATCH)]
            for j in range(BATCH):
                gath[pl.ds(k * NT + n + j, 1), :] = got[j]

    def add_members(tile):
        ids = jnp.concatenate(
            [pool[pl.ds(tile * (NT // 128) + j, 1), :] for j in range(NT // 128)], axis=1
        )
        rows = held[...]
        for c in range(0, groups * clusters, 256):
            names = lax.broadcasted_iota(jnp.int32, (256, NT), 0) + c
            acc[c:c + 256, :] += dot(jnp.where(names == ids, 1.0, 0.0).astype(BF16), rows)

    gather(0)
    p = dot(edge[...], ein[2])
    pre_lo[...] = p[:, :128]
    pre_hi[...] = p[:, 128:]
    own = node[...]
    rv = dot(own, ein[1]) + bias[0:1, :]
    add_members(jnp.maximum(step - 1, 0))
    total = jnp.zeros((NT, 256), F32)
    for k in range(DEG):
        if k + 1 < DEG:
            gather(k + 1)
        g = gath[k * NT:(k + 1) * NT, :]
        s = jnp.concatenate([(g << 16) >> 16, g >> 16], axis=1).astype(F32) * scale[...]
        e = jnp.concatenate(
            [pre_lo[pl.ds(k, NT, stride=DEG), :], pre_hi[pl.ds(k, NT, stride=DEG), :]], axis=1
        )
        h = jnp.maximum(e + s + rv, 0.0).astype(BF16)
        total = total + unit_rows(dot(h, eoc[...]) + bc[1:2, :])
    summed = (total * gain[0:1, :]).astype(BF16)
    h = jnp.maximum(dot(own, nin[0]) + dot(summed, nin[1]) + bias[2:3, :], 0.0).astype(BF16)
    update = unit_rows(dot(h, noc[...]) + bc[3:4, :]) * gain[1:2, :]
    result = (own.astype(F32) + update).astype(BF16)
    out[...] = result
    held[...] = result

    @pl.when(step == steps - 1)
    def _():
        add_members(step)
        for g in range(groups):
            c = g * clusters
            part[g, 0:clusters, :] = acc[c:c + clusters, :].astype(BF16)
            n = count[:, c:c + clusters]
            big = jnp.floor(n * (1.0 / 256.0)) * 256.0
            which = lax.broadcasted_iota(jnp.int32, (16, clusters), 0)
            part[g, clusters:clusters + 16, :] = jnp.where(
                which == 0, n - big, jnp.where(which == 1, big, 0.0)
            ).astype(BF16)


def fine_level(groups, clusters, send, pool, count, table, scale, node, edge, ein, eout, nin, nout, bias, gain):
    rows, width = node.shape
    steps = rows // NT
    et = NT * DEG
    whole = pl.BlockSpec(memory_space=pltpu.VMEM)
    return pl.pallas_call(
        functools.partial(fine_kernel, groups, clusters),
        grid=(steps,),
        in_specs=[pl.BlockSpec(memory_space=pltpu.SMEM), whole, whole, whole, whole,
                  pl.BlockSpec((NT, width), lambda i: (i, 0)),
                  pl.BlockSpec((et, width), lambda i: (i, 0))] + [whole] * 6,
        out_specs=[pl.BlockSpec((NT, width), lambda i: (i, 0)),
                   pl.BlockSpec((groups, clusters + 16, width), lambda i: (0, 0, 0))],
        out_shape=[jax.ShapeDtypeStruct((rows, width), BF16),
                   jax.ShapeDtypeStruct((groups, clusters + 16, width), BF16)],
        scratch_shapes=[
            pltpu.VMEM((et, 128), jnp.int32),
            pltpu.VMEM((et, 128), F32),
            pltpu.VMEM((et, 128), F32),
            pltpu.VMEM((width, width), BF16),
            pltpu.VMEM((width, width), BF16),
            pltpu.VMEM((4, width), F32),
            pltpu.VMEM((groups * clusters, width), F32),
            pltpu.VMEM((NT, width), BF16),
        ],
        compiler_params=pltpu.CompilerParams(vmem_limit_bytes=VMEM),
        cost_estimate=pl.CostEstimate(flops=7_000_000_000, bytes_accessed=9_000_000, transcendentals=0),
        name="fine_level",
    )(send, pool.reshape(-1, 128), count, table, scale, node, edge, ein, eout, nin, nout, bias, gain)


def coarse_kernel(
    part, lat_far, edge_far, sends, lists, ein_far, eout_far, nin_far, nout_far, bias, gain,
    out,
    mine_part, lat, edge, ein, eout, nin, nout, local,
    got, edges_lo, edges_hi, rim_out, rim_in, mix, names, near, far, chosen, sum_send, sum_recv, rim_send, rim_recv,
):
    groups = part.shape[0]
    rows, width = lat.shape
    rim = rim_in.shape[1]
    mine = lax.axis_index("group")
    here = lax.axis_index("dom")
    last = lax.axis_size("dom") - 1
    has_low = here > 0
    has_high = here < last
    below = jnp.maximum(here - 1, 0)
    above = jnp.minimum(here + 1, last)
    mesh_id = pl.DeviceIdType.MESH

    barrier = pltpu.get_barrier_semaphore()
    for o in range(1, groups):
        pl.semaphore_signal(
            barrier, inc=1, device_id=(lax.rem(mine + o, groups), here), device_id_type=mesh_id
        )

    @pl.when(has_low)
    def _():
        pl.semaphore_signal(barrier, inc=1, device_id=(mine, below), device_id_type=mesh_id)

    @pl.when(has_high)
    def _():
        pl.semaphore_signal(barrier, inc=1, device_id=(mine, above), device_id_type=mesh_id)

    loads = [
        pltpu.make_async_copy(source, target, local.at[i])
        for i, (source, target) in enumerate((
            (eout_far, eout), (nout_far, nout), (edge_far, edge), (ein_far, ein),
            (part.at[mine], mine_part), (lat_far, lat), (nin_far, nin),
        ))
    ]
    for load in loads:
        load.start()
    pl.semaphore_wait(barrier, groups - 1 + has_low.astype(jnp.int32) + has_high.astype(jnp.int32))
    copies = []
    for o in range(1, groups):
        peer = lax.rem(mine + o, groups)
        copy = pltpu.make_async_remote_copy(
            src_ref=part.at[peer], dst_ref=got.at[o - 1],
            send_sem=sum_send.at[o - 1], recv_sem=sum_recv.at[o - 1],
            device_id=(peer, here), device_id_type=mesh_id,
        )
        copy.start()
        copies.append(copy)

    for load in loads:
        load.wait()
    eoc = centre(eout[...])
    noc = centre(nout[...])
    b = bias[...]
    bc = b - jnp.mean(b, axis=-1, keepdims=True)
    for r in range(0, edge.shape[0], 256):
        p = dot(edge[r:r + 256, :], ein[2])
        edges_lo[r:r + 256, :] = p[:, :128]
        edges_hi[r:r + 256, :] = p[:, 128:]
    for r in range(sends.shape[0]):
        names[r * 128:(r + 1) * 128, :] = column(sends[r:r + 1, :])
    for k in range(DEG):
        at = names[pl.ds(k, rows, stride=DEG), :]
        near[k] = one_hot(at, range(rim, rim + rows, 128))
        far[k] = one_hot(
            at, list(range(0, rim, 128)) + list(range(rim + rows, 2 * rim + rows, 128))
        )
    picks = jnp.concatenate([column(lists[r:r + 1, :]) for r in range(lists.shape[0])], axis=0)
    chosen[...] = one_hot(picks, range(0, rows, 128))
    sums = mine_part[...].astype(F32)
    for copy in copies:
        copy.wait_recv()
    for o in range(1, groups):
        sums = sums + got[o - 1].astype(F32)
    members = sums[rows:rows + 1, :] + sums[rows + 1:rows + 2, :]
    inv = jnp.broadcast_to(1.0 / jnp.maximum(members, 1.0), (128, rows)).T
    inv = jnp.concatenate([inv] * (width // 128), axis=1)
    own = (lat[...].astype(F32) + sums[:rows, :] * inv).astype(BF16)
    border_rows = dot(chosen[...], own).astype(BF16)
    rim_out[0] = border_rows[:rim, :]
    rim_out[1] = border_rows[rim:, :]
    down = pltpu.make_async_remote_copy(
        src_ref=rim_out.at[0], dst_ref=rim_in.at[1],
        send_sem=rim_send.at[0], recv_sem=rim_recv.at[0],
        device_id=(mine, below), device_id_type=mesh_id,
    )
    up = pltpu.make_async_remote_copy(
        src_ref=rim_out.at[1], dst_ref=rim_in.at[0],
        send_sem=rim_send.at[1], recv_sem=rim_recv.at[1],
        device_id=(mine, above), device_id_type=mesh_id,
    )

    @pl.when(has_low)
    def _():
        down.start()

    @pl.when(has_high)
    def _():
        up.start()

    @pl.when(jnp.logical_not(has_low))
    def _():
        rim_in[0] = jnp.zeros((rim, width), BF16)

    @pl.when(jnp.logical_not(has_high))
    def _():
        rim_in[1] = jnp.zeros((rim, width), BF16)

    sender = dot(own, ein[0]).astype(BF16)
    recv = dot(own, ein[1]) + b[0:1, :]
    npre = dot(own, nin[0]) + b[2:3, :]
    for k in range(DEG):
        e = jnp.concatenate(
            [edges_lo[pl.ds(k, rows, stride=DEG), :], edges_hi[pl.ds(k, rows, stride=DEG), :]],
            axis=1,
        )
        mix[k] = e + recv + dot(near[k], sender)

    @pl.when(has_high)
    def _():
        down.wait_recv()

    @pl.when(has_low)
    def _():
        up.wait_recv()

    low = dot(rim_in[0], ein[0]).astype(BF16)
    high = dot(rim_in[1], ein[0]).astype(BF16)
    rims = jnp.concatenate([low, high], axis=0)
    total = jnp.zeros((rows, width), F32)
    for k in range(DEG):
        h = jnp.maximum(mix[k] + dot(far[k], rims), 0.0).astype(BF16)
        total = total + unit_rows(dot(h, eoc) + bc[1:2, :])
    summed = (total * gain[0:1, :]).astype(BF16)
    h = jnp.maximum(npre + dot(summed, nin[1]), 0.0).astype(BF16)
    update = unit_rows(dot(h, noc) + bc[3:4, :]) * gain[1:2, :]
    out[...] = own.astype(F32) + update
    for copy in copies:
        copy.wait_send()

    @pl.when(has_low)
    def _():
        down.wait_send()

    @pl.when(has_high)
    def _():
        up.wait_send()


def coarse_level(part, lat, edge, send, lists, ein, eout, nin, nout, bias, gain):
    groups = part.shape[0]
    rows, width = lat.shape
    rim = lists.shape[0] // 2
    far = pl.BlockSpec(memory_space=pl.ANY)
    near = pl.BlockSpec(memory_space=pltpu.VMEM)
    return pl.pallas_call(
        coarse_kernel,
        in_specs=[far, far, far, near, near, far, far, far, far, near, near],
        out_specs=pl.BlockSpec(memory_space=pltpu.VMEM),
        out_shape=jax.ShapeDtypeStruct((rows, width), F32),
        scratch_shapes=[
            pltpu.VMEM(part.shape[1:], BF16),
            pltpu.VMEM(lat.shape, BF16),
            pltpu.VMEM(edge.shape, BF16),
            pltpu.VMEM(ein.shape, BF16),
            pltpu.VMEM(eout.shape, BF16),
            pltpu.VMEM(nin.shape, BF16),
            pltpu.VMEM(nout.shape, BF16),
            pltpu.SemaphoreType.DMA((7,)),
            pltpu.VMEM((groups - 1,) + part.shape[1:], BF16),
            pltpu.VMEM((edge.shape[0], 128), F32),
            pltpu.VMEM((edge.shape[0], 128), F32),
            pltpu.VMEM((2, rim, width), BF16),
            pltpu.VMEM((2, rim, width), BF16),
            pltpu.VMEM((DEG, rows, width), F32),
            pltpu.VMEM((edge.shape[0], 128), jnp.int32),
            pltpu.VMEM((DEG, rows, rows), BF16),
            pltpu.VMEM((DEG, rows, 2 * rim), BF16),
            pltpu.VMEM((2 * rim, rows), BF16),
            pltpu.SemaphoreType.DMA((groups - 1,)),
            pltpu.SemaphoreType.DMA((groups - 1,)),
            pltpu.SemaphoreType.DMA((2,)),
            pltpu.SemaphoreType.DMA((2,)),
        ],
        compiler_params=pltpu.CompilerParams(
            vmem_limit_bytes=VMEM, collective_id=0, has_side_effects=True
        ),
        cost_estimate=pl.CostEstimate(flops=1_500_000_000, bytes_accessed=3_000_000, transcendentals=0),
        name="coarse_level",
    )(part, lat, edge, send.reshape(-1, 128), lists.reshape(-1, 128),
      ein, eout, nin, nout, bias, gain)


def body(
    node_lat, edge_lat, edge_send, halo_list, pool_id,
    coarse_lat, cedge_lat, cedge_send, chalo_list,
    fine_edge_in, fine_edge_out, fine_node_in, fine_node_out, fine_bias, fine_gain,
    coarse_edge_in, coarse_edge_out, coarse_node_in, coarse_node_out, coarse_bias, coarse_gain,
):
    groups = lax.axis_size("group")
    clusters, width = coarse_lat.shape
    table, scale, count = front(groups * clusters, halo_list, pool_id, node_lat, fine_edge_in)
    table = table.reshape(table.shape[0], 1, table.shape[1])
    fine_out, part = fine_level(
        groups, clusters, edge_send, pool_id, count, table, scale, node_lat, edge_lat,
        fine_edge_in, fine_edge_out, fine_node_in, fine_node_out, fine_bias, fine_gain,
    )
    coarse_out = coarse_level(
        part, coarse_lat, cedge_lat, cedge_send, chalo_list,
        coarse_edge_in, coarse_edge_out, coarse_node_in, coarse_node_out, coarse_bias, coarse_gain,
    )
    return (fine_out, coarse_out.astype(BF16))


def solution(mesh):
    both = ("group", "dom")
    rows, flat = P(both, None), P(both)
    placed = (rows, rows, flat, flat, flat, rows, rows, flat, flat) + (P(),) * 12
    return jax.shard_map(body, mesh=mesh, in_specs=placed, out_specs=(rows, rows), check_vma=False)
```
